32 devices in a mesh: grp: 16 (over z, y, x), fold: 2 (over core).
Axes of the slice: x: 2, y: 2, z: 4, core: 2. Of those that a mesh axis runs over, the one named last changes fastest.
Arguments:
- blocks: bfloat16 [9, 2, 64, 64, 2048], P(None, None, 'fold', None, 'grp'), may hold values from -30 to 30
- source: bfloat16 [2, 64, 12, 2048], P(None, 'fold', None, 'grp'), may hold values from -8 to 8
- plane_counts: int32 [16], P('grp'), may hold values from 1 to 2, 24 in all
Outputs:
- solution: float32 [2, 64, 12, 2048], P(None, 'fold', None, 'grp')
- residual: float32 [2, 64, 12, 2048], P(None, 'fold', None, 'grp')
The draws below stay inside these ranges and needn't reach their ends.
Inputs may be any that keep to these rules, and one draw needn't show every extreme that they name: plane_counts sum to 24; the busiest group holds exactly 2 planes.
All inputs are finite; a program needn't handle non-finite values.
Results may differ from the reference program's by a relative error of at most 0.0032.
Values may be sent and summed in bfloat16 or wider, within the bound.
A program may use at most 128 MiB of HBM per device.

```python
import math
import jax
import jax.numpy as jnp
import numpy as np

NCOMP = 64
NRHS = 12
LX = 4
LY = 4
LT = 4
SWEEPS = 2
CAP = 2
PLANE = 64
SITES = 2048
NZ = 24
N_GRP = 16


def draw_blocks(key, part):
    first_key = jax.random.fold_in(key, 11)
    second_key = jax.random.fold_in(key, 12)
    third_key = jax.random.fold_in(key, 13)
    fourth_key = jax.random.fold_in(key, 14)
    fifth_key = jax.random.fold_in(key, 15)
    shape_full = (9, 2, NCOMP, NCOMP, SITES)
    jitter = jax.random.truncated_normal(first_key, -4.0, 4.0, shape_full, jnp.float32)
    hop_scale = jnp.where(jnp.arange(9) == 0, 0.04, 0.015).astype(jnp.float32).reshape(9, 1, 1, 1, 1)
    diagonal = jax.random.uniform(second_key, (NCOMP, SITES), jnp.float32, 1.5, 3.0)
    diagonal_imag = jax.random.uniform(third_key, (NCOMP, SITES), jnp.float32, 0.0, 1.2)
    identity = jnp.eye(NCOMP, dtype=jnp.float32)
    result = jitter * hop_scale
    result = result.at[0, 0].add(identity[:, :, None] * diagonal[:, None, :])
    result = result.at[0, 1].add(identity[:, :, None] * diagonal_imag[:, None, :])
    groups = SITES // (CAP * PLANE)
    ramp = 1.0 + 2.0 * jnp.arange(groups).astype(jnp.float32) / max(groups - 1, 1)
    group_factor = jnp.exp(jax.random.uniform(fourth_key, (groups,), jnp.float32, math.log(0.6), math.log(1.6)))
    group_of = (jnp.arange(SITES) // (CAP * PLANE)).astype(jnp.int32)
    site_scale = (ramp * group_factor)[group_of]
    row_factor = jnp.exp(jax.random.uniform(fifth_key, (NCOMP,), jnp.float32, math.log(0.6), math.log(1.6)))
    return (result * site_scale.reshape(1, 1, 1, 1, SITES) * row_factor.reshape(1, 1, NCOMP, 1, 1)).astype(jnp.bfloat16)


def draw_source(key, part):
    first_key = jax.random.fold_in(key, 21)
    shape_full = (2, NCOMP, NRHS, SITES)
    return jax.random.truncated_normal(first_key, -5.0, 5.0, shape_full, jnp.float32).astype(jnp.bfloat16)


def split_up(count, total, most, lean):
    loads = [(1 << 20) // math.isqrt(rank ** lean) + 1 for rank in range(2, count + 1)]
    spare, counts = total - most - (count - 1), [1] * (count - 1)
    while spare > 0:
        movable = [i for i in range(count - 1) if counts[i] < most]
        whole, left = sum([loads[i] for i in movable]), spare
        for i in movable:
            extra = min(most - counts[i], max(1, left * loads[i] // whole), spare)
            counts[i] = counts[i] + extra
            spare = spare - extra
    return np.array([most] + counts)


def ragged(stream_key, amount, total, most, slope):
    if amount == 2:
        one = jax.random.randint(stream_key, (), max(1, total - most), min(most, total - 1) + 1)
        return jnp.stack([one, total - one])
    sizes = jnp.asarray(split_up(amount, total, most, slope), jnp.int32)
    twos = (amount - 1) // 2
    donor, taker = sizes[1:1 + 2 * twos:2], sizes[2:2 + 2 * twos:2]
    room = jnp.minimum(donor - 1, most - taker)
    passed = jax.random.randint(jax.random.fold_in(stream_key, 1), (twos,), 0, 1 << 20) % (room + 1)
    sizes = sizes.at[1:1 + 2 * twos:2].set(donor - passed).at[2:2 + 2 * twos:2].set(taker + passed)
    return sizes[jax.random.permutation(jax.random.fold_in(stream_key, 2), amount)]


def setup_inputs(seed: int = 0) -> dict:
    key_list = jax.random.split(jax.random.key(seed), 4)
    return {
        "blocks": draw_blocks(jax.random.fold_in(key_list[3], 71), 0),
        "source": draw_source(jax.random.fold_in(key_list[3], 71), 0),
        "plane_counts": ragged(key_list[2], N_GRP, NZ, CAP, 2).astype(jnp.int32),
    }


def complex_apply(block_pair, vector):
    first = block_pair[0].astype(jnp.float32)
    second = block_pair[1].astype(jnp.float32)
    vec_real = vector[0].astype(jnp.float32)
    vec_imag = vector[1].astype(jnp.float32)
    real_part = jnp.einsum("rcs,cks->rks", first, vec_real) - jnp.einsum("rcs,cks->rks", second, vec_imag)
    imag_part = jnp.einsum("rcs,cks->rks", first, vec_imag) + jnp.einsum("rcs,cks->rks", second, vec_real)
    return jnp.stack([real_part, imag_part])


def reference(blocks, source, plane_counts):
    group_count = plane_counts.shape[0]
    plane_sites = LX * LY * LT
    slot_index = jnp.arange(group_count * CAP).astype(jnp.int32)
    group_of = slot_index // CAP
    plane_slot = slot_index % CAP
    prior = (group_of - 1) % group_count
    later = (group_of + 1) % group_count
    lower_index = jnp.where(plane_slot > 0, slot_index - 1, prior * CAP + plane_counts[prior] - 1).astype(jnp.int32)
    upper_index = jnp.where(plane_slot < plane_counts[group_of] - 1, slot_index + 1, later * CAP).astype(jnp.int32)
    live_mask = jnp.repeat((plane_slot < plane_counts[group_of]).astype(jnp.float32), plane_sites)

    def operate(rounded):
        leading = rounded.shape[:3]
        flat_shape = leading + (group_count * CAP * plane_sites,)
        by_plane = rounded.reshape(leading + (group_count * CAP, plane_sites))
        lattice = rounded.reshape(leading + (group_count * CAP, LX, LY, LT))
        neighbours = [rounded]
        for axis_index in (4, 5):
            neighbours.append(jnp.roll(lattice, -1, axis_index).reshape(flat_shape))
            neighbours.append(jnp.roll(lattice, 1, axis_index).reshape(flat_shape))
        neighbours.append(jnp.take(by_plane, upper_index, axis=3).reshape(flat_shape))
        neighbours.append(jnp.take(by_plane, lower_index, axis=3).reshape(flat_shape))
        neighbours.append(jnp.roll(lattice, -1, 6).reshape(flat_shape))
        neighbours.append(jnp.roll(lattice, 1, 6).reshape(flat_shape))
        summed = complex_apply(blocks[0], neighbours[0])
        for hop_index in range(1, 9):
            summed = summed + complex_apply(blocks[hop_index], neighbours[hop_index])
        return summed * live_mask

    residual = source.astype(jnp.float32) * live_mask
    solution = jnp.zeros_like(residual)
    for sweep_index in range(SWEEPS):
        rounded = residual.astype(jnp.bfloat16)
        applied = operate(rounded)
        intersection_re = jnp.sum(applied[0] * residual[0] + applied[1] * residual[1], axis=(0, 2))
        intersection_im = jnp.sum(applied[0] * residual[1] - applied[1] * residual[0], axis=(0, 2))
        image_norm = jnp.sum(applied * applied, axis=(0, 1, 3))
        alpha_re = (intersection_re / image_norm)[:, None]
        alpha_im = (intersection_im / image_norm)[:, None]
        solution = solution + jnp.stack([alpha_re * residual[0] - alpha_im * residual[1], alpha_re * residual[1] + alpha_im * residual[0]])
        residual = residual - jnp.stack([alpha_re * applied[0] - alpha_im * applied[1], alpha_re * applied[1] + alpha_im * applied[0]])
    return solution, residual
```

```python
import functools

import jax
import jax.numpy as jnp
import numpy as np
from jax import lax
from jax.experimental import pallas as pl
from jax.experimental.pallas import tpu as pltpu
from jax.sharding import PartitionSpec as P

SWEEPS = 2
CHUNK = 8
GROUPS = 16
HALF = GROUPS // 2
LOCAL = (0, 1, 2, 3, 4, 7, 8)
ACROSS = (5, 6)
MESH = pl.DeviceIdType.MESH


def lane_moves():
    moves = np.zeros((256, 512), np.float32)
    for lane in range(128):
        base, site = lane // 8 * 8, lane % 8
        low = site < 4
        moves[base + (site ^ 4) + (0 if low else 128), lane] = 1
        moves[base + (site ^ 4) + (128 if low else 0), 128 + lane] = 1
        moves[base + (site & 4) + ((site + 1) & 3), 256 + lane] = 1
        moves[base + (site & 4) + ((site - 1) & 3), 384 + lane] = 1
    return jnp.asarray(moves, jnp.bfloat16)


def swap_blocks(tiles):
    tiles = list(tiles)
    block = lax.broadcasted_iota(jnp.int32, tiles[0].shape, 1) // CHUNK
    for bit in (1, 2, 4, 8):
        high = block // bit % 2 == 1
        for i in range(GROUPS):
            if i & bit == 0:
                a, b = tiles[i], tiles[i | bit]
                tiles[i] = jnp.where(high, pltpu.roll(b, CHUNK * bit, 1), a)
                tiles[i | bit] = jnp.where(high, b, pltpu.roll(a, 128 - CHUNK * bit, 1))
    return tiles


def turned(alpha_re, alpha_im, v):
    re, im = v[:, :128], v[:, 128:]
    return jnp.concatenate([alpha_re * re - alpha_im * im, alpha_re * im + alpha_im * re], axis=1)


def kernel(n_grp, n_fold, counts, blocks, source, moves, res_out, image_out, alphas,
           raw, w_local, w_across, image, res, first_image, gath, last, edge_image, rims, local_rhs, red,
           load_sem, x_send, x_recv, r_send, r_recv, s_send, s_recv):
    bf16, f32 = jnp.bfloat16, jnp.float32
    rows, comps = blocks.shape[2], blocks.shape[3]
    nrhs = source.shape[1]
    total = n_grp * n_fold
    grp, fold = lax.axis_index("grp"), lax.axis_index("fold")
    me = grp * n_fold + fold
    loads = [pltpu.make_async_copy(blocks.at[m], raw.at[m], load_sem.at[m]) for m in range(9)]
    for load in loads:
        load.start()

    def device(index):
        return (lax.div(index, n_fold), lax.rem(index, n_fold))

    barrier = pltpu.get_barrier_semaphore()

    def greet(d, carry):
        pl.semaphore_signal(barrier, inc=1, device_id=device(lax.rem(me + d, total)), device_id_type=MESH)
        return carry

    lax.fori_loop(1, total, greet, 0, unroll=total <= 64)

    live = (counts[0] - 1).astype(f32)

    for p in range(2):
        planes = [source[p, k].astype(f32) for k in range(nrhs)]
        for t in range(0, rows, 8):
            tiles = [plane[t:t + 8] for plane in planes]
            tiles += [jnp.zeros((8, 128), f32)] * (GROUPS - nrhs)
            for g, tile in enumerate(swap_blocks(tiles)):
                res[g, t:t + 8, 128 * p:128 * p + 128] = tile * live if g >= HALF else tile

    pl.semaphore_wait(barrier, total - 1)

    def exchange(sweep, mine, slots, first_plane, last_plane):
        copies = []
        for side, src, step in ((0, first_plane, n_grp - 1), (1, last_plane, 1)):
            copies.append(pltpu.make_async_remote_copy(
                src_ref=src, dst_ref=rims.at[sweep, side, fold],
                send_sem=r_send.at[sweep, side, 0], recv_sem=r_recv.at[sweep, side, 0],
                device_id=(lax.rem(grp + step, n_grp), fold), device_id_type=MESH))
        for d in range(1, n_fold):
            copies.append(pltpu.make_async_remote_copy(
                src_ref=mine, dst_ref=slots.at[fold],
                send_sem=x_send.at[sweep, d], recv_sem=x_recv.at[sweep, d],
                device_id=(grp, lax.rem(fold + d, n_fold)), device_id_type=MESH))
        for copy in copies:
            copy.start()
        return copies

    def send_source():
        def fill(h, carry):
            lower, upper = res[h], res[h + HALF]
            gath[fold, h] = lower.astype(bf16)
            gath[fold, h + HALF] = upper.astype(bf16)
            last[h] = (upper * live + lower * (1.0 - live)).astype(bf16)
            return carry

        lax.fori_loop(0, HALF, fill, 0, unroll=2)
        return exchange(0, gath.at[fold], gath, gath.at[fold, pl.ds(0, HALF)], last)

    def send_image():
        return exchange(1, first_image.at[fold], first_image, edge_image.at[0], edge_image.at[1])

    def wait_gather(sweep, slots):
        for d in range(1, n_fold):
            slot = slots.at[lax.rem(fold + n_fold - d, n_fold)]
            pltpu.make_async_remote_copy(
                src_ref=slot, dst_ref=slot, send_sem=x_send.at[sweep, d], recv_sem=x_recv.at[sweep, d],
                device_id=(grp, lax.rem(fold + d, n_fold)), device_id_type=MESH).wait_recv()

    def forward(sweep, side, d, sender):
        slot = rims.at[sweep, side, sender]
        return pltpu.make_async_remote_copy(
            src_ref=slot, dst_ref=slot, send_sem=r_send.at[sweep, side, d],
            recv_sem=r_recv.at[sweep, side, d],
            device_id=(grp, lax.rem(fold + d, n_fold)), device_id_type=MESH)

    def pass_edges(sweep, edges):
        passed = []
        for side in range(2):
            edges[side].wait_recv()
            passed += [forward(sweep, side, d, fold) for d in range(1, n_fold)]
            for copy in passed[-(n_fold - 1):]:
                copy.start()
        return passed

    def wait_edges(sweep):
        for side in range(2):
            for d in range(1, n_fold):
                forward(sweep, side, d, lax.rem(fold + n_fold - d, n_fold)).wait_recv()

    def whole_rows(read):
        parts = [read(f) for f in range(n_fold)]
        if rows % 16:
            return jnp.concatenate([part.astype(f32) for part in parts], axis=0).astype(bf16)
        return jnp.concatenate(parts, axis=0)

    def doubled(re, im):
        return jnp.concatenate(
            [jnp.concatenate([re, im], axis=1), jnp.concatenate([-im, re], axis=1)], axis=0)

    def stepped(alpha, start, moved):
        parts = [start(f).astype(f32) - turned(*alpha, moved(f).astype(f32)) for f in range(n_fold)]
        return jnp.concatenate(parts, axis=0).astype(bf16)

    def build_local(alpha):
        def pair(h, carry):
            if alpha is None:
                chunks = [whole_rows(lambda f, i=i: gath[f, 2 * h + i]) for i in range(2)]
            else:
                chunks = []
                for g in (2 * h, 2 * h + 1):
                    res[g] = res[g] - turned(*alpha, first_image[fold, g])
                    chunks.append(stepped(alpha, lambda f, g=g: gath[f, g], lambda f, g=g: first_image[f, g]))
            (are, aim), (bre, bim) = [(c[:, :128], c[:, 128:]) for c in chunks]
            local_rhs[0, 2 * h] = doubled(are, aim)
            local_rhs[0, 2 * h + 1] = doubled(bre, bim)
            left = jnp.concatenate([jnp.concatenate([are, aim, bre, bim], axis=0),
                                    jnp.concatenate([bre, bim, are, aim], axis=0)], axis=1)
            moved = jnp.dot(left, moves[...], preferred_element_type=f32).astype(bf16)
            for i in range(2):
                for hop in range(4):
                    cut = moved[2 * comps * i:2 * comps * (i + 1), 128 * hop:128 * hop + 128]
                    local_rhs[1 + hop, 2 * h + i] = doubled(cut[:comps], cut[comps:])
            return carry

        lax.fori_loop(0, HALF, pair, 0, unroll=2)

    row_site = lax.broadcasted_iota(jnp.int32, (rows * CHUNK, 256), 0) % CHUNK
    lane_site = lax.broadcasted_iota(jnp.int32, (rows * CHUNK, 256), 1) % CHUNK

    def same_site(product):
        kept = jnp.where(row_site == lane_site, product, 0.0)
        return jnp.sum(kept.reshape(rows, CHUNK, 256), axis=1)

    def apply_local(begin, end):
        def chunk(g, carry):
            plane, x, low = g // HALF * HALF, g % HALF // 2, g % 2
            ahead, behind = plane + (x + 1) % 4 * 2 + low, plane + (x + 3) % 4 * 2 + low
            rhs = jnp.concatenate(
                [local_rhs[0, g], local_rhs[0, ahead], local_rhs[0, behind]]
                + [local_rhs[1 + hop, g] for hop in range(4)], axis=0)
            image[g] = same_site(jnp.dot(w_local[g], rhs, preferred_element_type=f32))
            return carry

        lax.fori_loop(begin, end, chunk, 0, unroll=8)

    def dots(a, r):
        are, aim, rre, rim = a[:, :128], a[:, 128:], r[:, :128], r[:, 128:]
        return are * rre + aim * rim, are * rim - aim * rre, are * are + aim * aim

    def apply_across(alpha):
        def plane_chunk(h, sums):
            if alpha is None:
                after, before = [whole_rows(lambda f, side=side: rims[0, side, f, h]) for side in range(2)]
            else:
                after, before = [stepped(alpha, lambda f, side=side: rims[0, side, f, h],
                                         lambda f, side=side: rims[1, side, f, h]) for side in range(2)]
            after = doubled(after[:, :128], after[:, 128:])
            before = doubled(before[:, :128], before[:, 128:])
            inner, outer = local_rhs[0, h], local_rhs[0, h + HALF]
            up = (outer.astype(f32) * live + after.astype(f32) * (1.0 - live)).astype(bf16)
            first = same_site(jnp.dot(w_across[h], jnp.concatenate([up, before], axis=0),
                                      preferred_element_type=f32))
            second = same_site(jnp.dot(w_across[h + HALF], jnp.concatenate([after, inner], axis=0),
                                       preferred_element_type=f32))
            first = first + image[h]
            second = (second + image[h + HALF]) * live
            if alpha is None:
                first_image[fold, h] = first
                first_image[fold, h + HALF] = second
                edge_image[0, h] = first.astype(bf16)
                edge_image[1, h] = (second + first * (1.0 - live)).astype(bf16)
            else:
                image[h] = first
                image[h + HALF] = second
            one, two = dots(first, res[h]), dots(second, res[h + HALF])
            return tuple(s + a + b for s, a, b in zip(sums, one, two))

        zero = jnp.zeros((rows, 128), f32)
        return lax.fori_loop(0, HALF, plane_chunk, (zero, zero, zero), unroll=4)

    row8 = lax.broadcasted_iota(jnp.int32, (8, 128), 0)
    lane8 = lax.broadcasted_iota(jnp.int32, (8, 128), 1)

    def spread(value):
        for step in (4, 2, 1):
            value = value + jnp.where(lane8 // step % 2 == 0,
                                      pltpu.roll(value, 128 - step, 1), pltpu.roll(value, step, 1))
        return value

    def send_sums(sweep, sums):
        re, im, norm = [jnp.sum(s, axis=0, keepdims=True) for s in sums]
        value = spread(jnp.where(row8 == 0, re, jnp.where(row8 == 1, im, norm)))
        spot = lane8[:1] % CHUNK
        red[sweep, 0] = jnp.where(spot == 0, value[0:1], jnp.where(spot == 1, value[1:2], value[2:3]))

        def send(d, carry):
            pltpu.make_async_remote_copy(
                src_ref=red.at[sweep, 0], dst_ref=red.at[sweep, d],
                send_sem=s_send.at[sweep], recv_sem=s_recv.at[sweep],
                device_id=device(lax.rem(me + d, total)), device_id_type=MESH).start()
            return carry

        lax.fori_loop(1, total, send, 0, unroll=total <= 64)

    def wait_sums(sweep):
        everyone = red.at[sweep, pl.ds(1, total - 1)]
        pltpu.make_async_copy(everyone, everyone, s_recv.at[sweep]).wait()
        value = jnp.broadcast_to(jnp.sum(red[sweep], axis=0), (8, 128))
        value = spread(jnp.where(lane8 % CHUNK == row8, value, 0.0))
        norm = jnp.where(lane8[:1] < CHUNK * nrhs, value[2:3], 1.0)
        return value[0:1] / norm, value[1:2] / norm

    def natural(held, out):
        for p in range(2):
            for t in range(0, rows, 8):
                tiles = swap_blocks([held[g, t:t + 8, 128 * p:128 * p + 128] for g in range(GROUPS)])
                for k in range(nrhs):
                    out[p, k, t:t + 8] = tiles[k]

    copies = send_source()
    for m in range(9):
        loads[m].wait()
        place = LOCAL.index(m) if m in LOCAL else ACROSS.index(m)
        target = w_local if m in LOCAL else w_across

        def two_rows(i, carry, m=m, place=place, target=target):
            flipped = []
            for a in range(2):
                both = jnp.concatenate([raw[m, 0, 2 * i + a], raw[m, 1, 2 * i + a]], axis=0)
                flipped.append(both.T.astype(f32))
            for g in range(GROUPS):
                piece = jnp.concatenate([f[8 * g:8 * g + 8] for f in flipped], axis=0)
                target[g, pl.ds(pl.multiple_of(16 * i, 16), 16),
                       2 * comps * place:2 * comps * (place + 1)] = piece.astype(bf16)
            return carry

        lax.fori_loop(0, rows // 2, two_rows, 0, unroll=min(rows // 2, 8))
    copies += pass_edges(0, copies[:2])
    wait_gather(0, gath)
    build_local(None)
    apply_local(0, GROUPS)
    wait_edges(0)
    send_sums(0, apply_across(None))
    later = send_image()
    first = wait_sums(0)
    wait_gather(1, first_image)
    build_local(first)
    apply_local(0, HALF)
    later += pass_edges(1, later[:2])
    apply_local(HALF, GROUPS)
    wait_edges(1)
    send_sums(1, apply_across(first))
    natural(res, res_out)
    natural(image, image_out)
    second = wait_sums(1)
    alphas[...] = jnp.where(row8 == 0, first[0], jnp.where(row8 == 1, first[1], jnp.where(
        row8 == 2, second[0], second[1])))
    for copy in copies + later:
        copy.wait_send()
    for sweep in range(SWEEPS):
        everyone = red.at[sweep, pl.ds(1, total - 1)]
        pltpu.make_async_copy(everyone, everyone, s_send.at[sweep]).wait()


def finish(counts, source, res, image, alphas, sol_out, res_out):
    nrhs, rows = source.shape[1:3]
    f32 = jnp.float32
    live = (counts[0] - 1).astype(f32)
    lane = lax.broadcasted_iota(jnp.int32, (rows, 128), 1)
    kept = jnp.where(lane < 64, 1.0, live)
    for k in range(nrhs):
        are, aim, bre, bim = [jnp.broadcast_to(alphas[i:i + 1, CHUNK * k:CHUNK * k + 1], (rows, 128))
                              for i in range(4)]
        sre, sim = [source[p, k].astype(f32) * kept for p in range(2)]
        rre, rim, ire, iim = res[0, k], res[1, k], image[0, k], image[1, k]
        sol_out[0, k] = (are * sre - aim * sim) + (bre * rre - bim * rim)
        sol_out[1, k] = (are * sim + aim * sre) + (bre * rim + bim * rre)
        res_out[0, k] = rre - (bre * ire - bim * iim)
        res_out[1, k] = rim - (bre * iim + bim * ire)


def body(n_grp, n_fold, blocks, source, plane_counts):
    rows, comps = blocks.shape[2], blocks.shape[3]
    nrhs = source.shape[2]
    bf16, f32 = jnp.bfloat16, jnp.float32
    shape = (2, nrhs, rows, GROUPS * CHUNK)
    vmem = pl.BlockSpec(memory_space=pltpu.VMEM)
    total = n_grp * n_fold
    held = jax.ShapeDtypeStruct(shape, f32)
    smem = pl.BlockSpec(memory_space=pltpu.SMEM)
    source = source.transpose(0, 2, 1, 3)
    iterate = pl.pallas_call(
        functools.partial(kernel, n_grp, n_fold),
        out_shape=(held, held, jax.ShapeDtypeStruct((8, 128), f32)),
        in_specs=[smem, pl.BlockSpec(memory_space=pl.ANY), vmem, vmem],
        out_specs=(vmem, vmem, vmem),
        scratch_shapes=[
            pltpu.VMEM(blocks.shape, bf16),
            pltpu.VMEM((GROUPS, rows * CHUNK, len(LOCAL) * 2 * comps), bf16),
            pltpu.VMEM((GROUPS, rows * CHUNK, len(ACROSS) * 2 * comps), bf16),
            pltpu.VMEM((GROUPS, rows, 256), f32),
            pltpu.VMEM((GROUPS, rows, 256), f32),
            pltpu.VMEM((n_fold, GROUPS, rows, 256), f32),
            pltpu.VMEM((n_fold, GROUPS, rows, 256), bf16),
            pltpu.VMEM((HALF, rows, 256), bf16),
            pltpu.VMEM((2, HALF, rows, 256), bf16),
            pltpu.VMEM((SWEEPS, 2, n_fold, HALF, rows, 256), bf16),
            pltpu.VMEM((5, GROUPS, 2 * comps, 256), bf16),
            pltpu.VMEM((SWEEPS, total, 1, 128), f32),
            pltpu.SemaphoreType.DMA((9,)),
            pltpu.SemaphoreType.DMA((SWEEPS, n_fold)),
            pltpu.SemaphoreType.DMA((SWEEPS, n_fold)),
            pltpu.SemaphoreType.DMA((SWEEPS, 2, n_fold)),
            pltpu.SemaphoreType.DMA((SWEEPS, 2, n_fold)),
            pltpu.SemaphoreType.DMA((SWEEPS,)),
            pltpu.SemaphoreType.DMA((SWEEPS,)),
        ],
        compiler_params=pltpu.CompilerParams(
            collective_id=0, has_side_effects=True, vmem_limit_bytes=56 * 1024 * 1024),
    )(plane_counts, blocks, source, lane_moves())
    outs = pl.pallas_call(
        finish,
        out_shape=(jax.ShapeDtypeStruct(shape, f32), jax.ShapeDtypeStruct(shape, f32)),
        in_specs=[smem, vmem, vmem, vmem, vmem],
        out_specs=(vmem, vmem),
        compiler_params=pltpu.CompilerParams(vmem_limit_bytes=8 * 1024 * 1024),
    )(plane_counts, source, *iterate)
    return tuple(out.transpose(0, 2, 1, 3) for out in outs)


def solution(mesh):
    return jax.shard_map(
        functools.partial(body, mesh.shape["grp"], mesh.shape["fold"]),
        mesh=mesh,
        in_specs=(P(None, None, "fold", None, "grp"), P(None, "fold", None, "grp"), P("grp")),
        out_specs=(P(None, "fold", None, "grp"), P(None, "fold", None, "grp")),
        check_vma=False,
    )
```

```python
import functools

import jax
import jax.numpy as jnp
import numpy as np
from jax import lax
from jax.experimental import pallas as pl
from jax.experimental.pallas import tpu as pltpu
from jax.sharding import PartitionSpec as P

SWEEPS = 2
CHUNK = 8
GROUPS = 16
HALF = GROUPS // 2
LOCAL = (0, 1, 2, 3, 4, 7, 8)
ACROSS = (5, 6)
MESH = pl.DeviceIdType.MESH


def lane_moves(hop):
    row = lax.broadcasted_iota(jnp.int32, (256, 128), 0)
    lane = lax.broadcasted_iota(jnp.int32, (256, 128), 1)
    base, site = lane // 8 * 8, lane % 8
    low, plane = site // 4 == 0, site // 4 * 4
    across = base + (site + 4) % 8
    origin = (jnp.where(low, across, across + 128), jnp.where(low, across + 128, across),
              base + plane + (site + 1) % 4, base + plane + (site + 3) % 4)[hop]
    return jnp.where(row == origin, 1.0, 0.0).astype(jnp.bfloat16)


def swap_blocks(tiles):
    tiles = list(tiles)
    block = lax.broadcasted_iota(jnp.int32, tiles[0].shape, 1) // CHUNK
    for bit in (1, 2, 4, 8):
        high = block // bit % 2 == 1
        for i in range(GROUPS):
            if i & bit == 0:
                a, b = tiles[i], tiles[i | bit]
                tiles[i] = jnp.where(high, pltpu.roll(b, CHUNK * bit, 1), a)
                tiles[i | bit] = jnp.where(high, b, pltpu.roll(a, 128 - CHUNK * bit, 1))
    return tiles


def turned(alpha_re, alpha_im, v):
    re, im = v[:, :128], v[:, 128:]
    return jnp.concatenate([alpha_re * re - alpha_im * im, alpha_re * im + alpha_im * re], axis=1)


def kernel(n_grp, n_fold, counts, blocks, source, res_out, image_out, alphas,
           moves, raw, w_local, w_across, image, res, first_image, gath, last, edge_image, rims, local_rhs, red,
           load_sem, x_send, x_recv, r_send, r_recv, s_send, s_recv):
    bf16, f32 = jnp.bfloat16, jnp.float32
    rows, comps = blocks.shape[2], blocks.shape[3]
    nrhs = source.shape[1]
    total = n_grp * n_fold
    grp, fold = lax.axis_index("grp"), lax.axis_index("fold")
    me = grp * n_fold + fold
    loads = [pltpu.make_async_copy(blocks.at[m], raw.at[m], load_sem.at[m]) for m in range(9)]
    for load in loads:
        load.start()

    def device(index):
        return (lax.div(index, n_fold), lax.rem(index, n_fold))

    barrier = pltpu.get_barrier_semaphore()

    def greet(d, carry):
        pl.semaphore_signal(barrier, inc=1, device_id=device(lax.rem(me + d, total)), device_id_type=MESH)
        return carry

    lax.fori_loop(1, total, greet, 0, unroll=total <= 64)

    live = (counts[0] - 1).astype(f32)

    for p in range(2):
        planes = [source[p, k].astype(f32) for k in range(nrhs)]
        for t in range(0, rows, 8):
            tiles = [plane[t:t + 8] for plane in planes]
            tiles += [jnp.zeros((8, 128), f32)] * (GROUPS - nrhs)
            for g, tile in enumerate(swap_blocks(tiles)):
                res[g, t:t + 8, 128 * p:128 * p + 128] = tile * live if g >= HALF else tile

    pl.semaphore_wait(barrier, total - 1)

    def exchange(sweep, mine, slots, first_plane, last_plane):
        copies = []
        for side, src, step in ((0, first_plane, n_grp - 1), (1, last_plane, 1)):
            copies.append(pltpu.make_async_remote_copy(
                src_ref=src, dst_ref=rims.at[sweep, side, fold],
                send_sem=r_send.at[sweep, side, 0], recv_sem=r_recv.at[sweep, side, 0],
                device_id=(lax.rem(grp + step, n_grp), fold), device_id_type=MESH))
        for d in range(1, n_fold):
            copies.append(pltpu.make_async_remote_copy(
                src_ref=mine, dst_ref=slots.at[fold],
                send_sem=x_send.at[sweep, d], recv_sem=x_recv.at[sweep, d],
                device_id=(grp, lax.rem(fold + d, n_fold)), device_id_type=MESH))
        for copy in copies:
            copy.start()
        return copies

    def send_source():
        def fill(h, carry):
            lower, upper = res[h], res[h + HALF]
            gath[fold, h] = lower.astype(bf16)
            gath[fold, h + HALF] = upper.astype(bf16)
            last[h] = (upper * live + lower * (1.0 - live)).astype(bf16)
            return carry

        lax.fori_loop(0, HALF, fill, 0, unroll=2)
        return exchange(0, gath.at[fold], gath, gath.at[fold, pl.ds(0, HALF)], last)

    def send_image():
        return exchange(1, first_image.at[fold], first_image, edge_image.at[0], edge_image.at[1])

    def wait_gather(sweep, slots):
        for d in range(1, n_fold):
            slot = slots.at[lax.rem(fold + n_fold - d, n_fold)]
            pltpu.make_async_remote_copy(
                src_ref=slot, dst_ref=slot, send_sem=x_send.at[sweep, d], recv_sem=x_recv.at[sweep, d],
                device_id=(grp, lax.rem(fold + d, n_fold)), device_id_type=MESH).wait_recv()

    def forward(sweep, side, d, sender):
        slot = rims.at[sweep, side, sender]
        return pltpu.make_async_remote_copy(
            src_ref=slot, dst_ref=slot, send_sem=r_send.at[sweep, side, d],
            recv_sem=r_recv.at[sweep, side, d],
            device_id=(grp, lax.rem(fold + d, n_fold)), device_id_type=MESH)

    def pass_edges(sweep, edges):
        passed = []
        for side in range(2):
            edges[side].wait_recv()
            passed += [forward(sweep, side, d, fold) for d in range(1, n_fold)]
            for copy in passed[-(n_fold - 1):]:
                copy.start()
        return passed

    def wait_edges(sweep):
        for side in range(2):
            for d in range(1, n_fold):
                forward(sweep, side, d, lax.rem(fold + n_fold - d, n_fold)).wait_recv()

    def whole_rows(read):
        parts = [read(f) for f in range(n_fold)]
        if rows % 16:
            return jnp.concatenate([part.astype(f32) for part in parts], axis=0).astype(bf16)
        return jnp.concatenate(parts, axis=0)

    def doubled(re, im):
        return jnp.concatenate(
            [jnp.concatenate([re, im], axis=1), jnp.concatenate([-im, re], axis=1)], axis=0)

    def stepped(alpha, start, moved):
        parts = [start(f).astype(f32) - turned(*alpha, moved(f).astype(f32)) for f in range(n_fold)]
        return jnp.concatenate(parts, axis=0).astype(bf16)

    def build_local(alpha):
        def pair(h, carry):
            if alpha is None:
                chunks = [whole_rows(lambda f, i=i: gath[f, 2 * h + i]) for i in range(2)]
            else:
                chunks = []
                for g in (2 * h, 2 * h + 1):
                    res[g] = res[g] - turned(*alpha, first_image[fold, g])
                    chunks.append(stepped(alpha, lambda f, g=g: gath[f, g], lambda f, g=g: first_image[f, g]))
            (are, aim), (bre, bim) = [(c[:, :128], c[:, 128:]) for c in chunks]
            local_rhs[0, 2 * h] = doubled(are, aim)
            local_rhs[0, 2 * h + 1] = doubled(bre, bim)
            left = jnp.concatenate([jnp.concatenate([are, aim, bre, bim], axis=0),
                                    jnp.concatenate([bre, bim, are, aim], axis=0)], axis=1)
            moved = jnp.dot(left, moves[...], preferred_element_type=f32).astype(bf16)
            for i in range(2):
                for hop in range(4):
                    cut = moved[2 * comps * i:2 * comps * (i + 1), 128 * hop:128 * hop + 128]
                    local_rhs[1 + hop, 2 * h + i] = doubled(cut[:comps], cut[comps:])
            return carry

        lax.fori_loop(0, HALF, pair, 0, unroll=2)

    row_site = lax.broadcasted_iota(jnp.int32, (rows * CHUNK, 256), 0) % CHUNK
    lane_site = lax.broadcasted_iota(jnp.int32, (rows * CHUNK, 256), 1) % CHUNK

    def same_site(product):
        kept = jnp.where(row_site == lane_site, product, 0.0)
        return jnp.sum(kept.reshape(rows, CHUNK, 256), axis=1)

    def apply_local(begin, end):
        def chunk(g, carry):
            plane, x, low = g // HALF * HALF, g % HALF // 2, g % 2
            ahead, behind = plane + (x + 1) % 4 * 2 + low, plane + (x + 3) % 4 * 2 + low
            rhs = jnp.concatenate(
                [local_rhs[0, g], local_rhs[0, ahead], local_rhs[0, behind]]
                + [local_rhs[1 + hop, g] for hop in range(4)], axis=0)
            image[g] = same_site(jnp.dot(w_local[g], rhs, preferred_element_type=f32))
            return carry

        lax.fori_loop(begin, end, chunk, 0, unroll=8)

    def dots(a, r):
        are, aim, rre, rim = a[:, :128], a[:, 128:], r[:, :128], r[:, 128:]
        return are * rre + aim * rim, are * rim - aim * rre, are * are + aim * aim

    def apply_across(alpha):
        def plane_chunk(h, sums):
            if alpha is None:
                after, before = [whole_rows(lambda f, side=side: rims[0, side, f, h]) for side in range(2)]
            else:
                after, before = [stepped(alpha, lambda f, side=side: rims[0, side, f, h],
                                         lambda f, side=side: rims[1, side, f, h]) for side in range(2)]
            after = doubled(after[:, :128], after[:, 128:])
            before = doubled(before[:, :128], before[:, 128:])
            inner, outer = local_rhs[0, h], local_rhs[0, h + HALF]
            up = (outer.astype(f32) * live + after.astype(f32) * (1.0 - live)).astype(bf16)
            first = same_site(jnp.dot(w_across[h], jnp.concatenate([up, before], axis=0),
                                      preferred_element_type=f32))
            second = same_site(jnp.dot(w_across[h + HALF], jnp.concatenate([after, inner], axis=0),
                                       preferred_element_type=f32))
            first = first + image[h]
            second = (second + image[h + HALF]) * live
            if alpha is None:
                first_image[fold, h] = first
                first_image[fold, h + HALF] = second
                edge_image[0, h] = first.astype(bf16)
                edge_image[1, h] = (second + first * (1.0 - live)).astype(bf16)
            else:
                image[h] = first
                image[h + HALF] = second
            one, two = dots(first, res[h]), dots(second, res[h + HALF])
            return tuple(s + a + b for s, a, b in zip(sums, one, two))

        zero = jnp.zeros((rows, 128), f32)
        return lax.fori_loop(0, HALF, plane_chunk, (zero, zero, zero), unroll=4)

    row8 = lax.broadcasted_iota(jnp.int32, (8, 128), 0)
    lane8 = lax.broadcasted_iota(jnp.int32, (8, 128), 1)

    def spread(value):
        for step in (4, 2, 1):
            value = value + jnp.where(lane8 // step % 2 == 0,
                                      pltpu.roll(value, 128 - step, 1), pltpu.roll(value, step, 1))
        return value

    def send_sums(sweep, sums):
        re, im, norm = [jnp.sum(s, axis=0, keepdims=True) for s in sums]
        value = spread(jnp.where(row8 == 0, re, jnp.where(row8 == 1, im, norm)))
        spot = lane8[:1] % CHUNK
        red[sweep, 0] = jnp.where(spot == 0, value[0:1], jnp.where(spot == 1, value[1:2], value[2:3]))

        def send(d, carry):
            pltpu.make_async_remote_copy(
                src_ref=red.at[sweep, 0], dst_ref=red.at[sweep, d],
                send_sem=s_send.at[sweep], recv_sem=s_recv.at[sweep],
                device_id=device(lax.rem(me + d, total)), device_id_type=MESH).start()
            return carry

        lax.fori_loop(1, total, send, 0, unroll=total <= 64)

    def wait_sums(sweep):
        everyone = red.at[sweep, pl.ds(1, total - 1)]
        pltpu.make_async_copy(everyone, everyone, s_recv.at[sweep]).wait()
        value = jnp.broadcast_to(jnp.sum(red[sweep], axis=0), (8, 128))
        value = spread(jnp.where(lane8 % CHUNK == row8, value, 0.0))
        norm = jnp.where(lane8[:1] < CHUNK * nrhs, value[2:3], 1.0)
        return value[0:1] / norm, value[1:2] / norm

    def natural(held, out):
        for p in range(2):
            for t in range(0, rows, 8):
                tiles = swap_blocks([held[g, t:t + 8, 128 * p:128 * p + 128] for g in range(GROUPS)])
                for k in range(nrhs):
                    out[p, k, t:t + 8] = tiles[k]

    copies = send_source()
    for hop in range(4):
        moves[:, 128 * hop:128 * hop + 128] = lane_moves(hop)
    for m in range(9):
        loads[m].wait()
        place = LOCAL.index(m) if m in LOCAL else ACROSS.index(m)
        target = w_local if m in LOCAL else w_across

        def two_rows(i, carry, m=m, place=place, target=target):
            flipped = []
            for a in range(2):
                both = jnp.concatenate([raw[m, 0, 2 * i + a], raw[m, 1, 2 * i + a]], axis=0)
                flipped.append(both.T.astype(f32))
            for g in range(GROUPS):
                piece = jnp.concatenate([f[8 * g:8 * g + 8] for f in flipped], axis=0)
                target[g, pl.ds(pl.multiple_of(16 * i, 16), 16),
                       2 * comps * place:2 * comps * (place + 1)] = piece.astype(bf16)
            return carry

        lax.fori_loop(0, rows // 2, two_rows, 0, unroll=min(rows // 2, 8))
    copies += pass_edges(0, copies[:2])
    wait_gather(0, gath)
    build_local(None)
    apply_local(0, GROUPS)
    wait_edges(0)
    send_sums(0, apply_across(None))
    later = send_image()
    first = wait_sums(0)
    wait_gather(1, first_image)
    build_local(first)
    apply_local(0, HALF)
    later += pass_edges(1, later[:2])
    apply_local(HALF, GROUPS)
    wait_edges(1)
    send_sums(1, apply_across(first))
    natural(res, res_out)
    natural(image, image_out)
    second = wait_sums(1)
    alphas[...] = jnp.where(row8 == 0, first[0], jnp.where(row8 == 1, first[1], jnp.where(
        row8 == 2, second[0], jnp.where(row8 == 3, second[1], jnp.where(lane8 < 64, 1.0, live)))))
    for copy in copies + later:
        copy.wait_send()
    for sweep in range(SWEEPS):
        everyone = red.at[sweep, pl.ds(1, total - 1)]
        pltpu.make_async_copy(everyone, everyone, s_send.at[sweep]).wait()


def finish(source, res, image, alphas, sol_out, res_out):
    nrhs, rows = source.shape[1:3]
    f32 = jnp.float32
    kept = jnp.broadcast_to(alphas[4:5], (rows, 128))
    for k in range(nrhs):
        are, aim, bre, bim = [jnp.broadcast_to(alphas[i:i + 1, CHUNK * k:CHUNK * k + 1], (rows, 128))
                              for i in range(4)]
        sre, sim = [source[p, k].astype(f32) * kept for p in range(2)]
        rre, rim, ire, iim = res[0, k], res[1, k], image[0, k], image[1, k]
        sol_out[0, k] = (are * sre - aim * sim) + (bre * rre - bim * rim)
        sol_out[1, k] = (are * sim + aim * sre) + (bre * rim + bim * rre)
        res_out[0, k] = rre - (bre * ire - bim * iim)
        res_out[1, k] = rim - (bre * iim + bim * ire)


def body(n_grp, n_fold, blocks, source, plane_counts):
    rows, comps = blocks.shape[2], blocks.shape[3]
    nrhs = source.shape[2]
    bf16, f32 = jnp.bfloat16, jnp.float32
    shape = (2, nrhs, rows, GROUPS * CHUNK)
    vmem = pl.BlockSpec(memory_space=pltpu.VMEM)
    total = n_grp * n_fold
    held = jax.ShapeDtypeStruct(shape, f32)
    smem = pl.BlockSpec(memory_space=pltpu.SMEM)
    source = source.transpose(0, 2, 1, 3)
    iterate = pl.pallas_call(
        functools.partial(kernel, n_grp, n_fold),
        out_shape=(held, held, jax.ShapeDtypeStruct((8, 128), f32)),
        in_specs=[smem, pl.BlockSpec(memory_space=pl.ANY), vmem],
        out_specs=(vmem, vmem, vmem),
        scratch_shapes=[
            pltpu.VMEM((256, 512), bf16),
            pltpu.VMEM(blocks.shape, bf16),
            pltpu.VMEM((GROUPS, rows * CHUNK, len(LOCAL) * 2 * comps), bf16),
            pltpu.VMEM((GROUPS, rows * CHUNK, len(ACROSS) * 2 * comps), bf16),
            pltpu.VMEM((GROUPS, rows, 256), f32),
            pltpu.VMEM((GROUPS, rows, 256), f32),
            pltpu.VMEM((n_fold, GROUPS, rows, 256), f32),
            pltpu.VMEM((n_fold, GROUPS, rows, 256), bf16),
            pltpu.VMEM((HALF, rows, 256), bf16),
            pltpu.VMEM((2, HALF, rows, 256), bf16),
            pltpu.VMEM((SWEEPS, 2, n_fold, HALF, rows, 256), bf16),
            pltpu.VMEM((5, GROUPS, 2 * comps, 256), bf16),
            pltpu.VMEM((SWEEPS, total, 1, 128), f32),
            pltpu.SemaphoreType.DMA((9,)),
            pltpu.SemaphoreType.DMA((SWEEPS, n_fold)),
            pltpu.SemaphoreType.DMA((SWEEPS, n_fold)),
            pltpu.SemaphoreType.DMA((SWEEPS, 2, n_fold)),
            pltpu.SemaphoreType.DMA((SWEEPS, 2, n_fold)),
            pltpu.SemaphoreType.DMA((SWEEPS,)),
            pltpu.SemaphoreType.DMA((SWEEPS,)),
        ],
        compiler_params=pltpu.CompilerParams(
            collective_id=0, has_side_effects=True, vmem_limit_bytes=52 * 1024 * 1024),
    )(plane_counts, blocks, source)
    outs = pl.pallas_call(
        finish,
        out_shape=(jax.ShapeDtypeStruct(shape, f32), jax.ShapeDtypeStruct(shape, f32)),
        in_specs=[vmem] * 4,
        out_specs=(vmem, vmem),
        compiler_params=pltpu.CompilerParams(vmem_limit_bytes=8 * 1024 * 1024),
    )(source, *iterate)
    return tuple(out.transpose(0, 2, 1, 3) for out in outs)


def solution(mesh):
    return jax.shard_map(
        functools.partial(body, mesh.shape["grp"], mesh.shape["fold"]),
        mesh=mesh,
        in_specs=(P(None, None, "fold", None, "grp"), P(None, "fold", None, "grp"), P("grp")),
        out_specs=(P(None, "fold", None, "grp"), P(None, "fold", None, "grp")),
        check_vma=False,
    )
```

```python
import functools

import jax
import jax.numpy as jnp
import numpy as np
from jax import lax
from jax.experimental import pallas as pl
from jax.experimental.pallas import tpu as pltpu
from jax.sharding import PartitionSpec as P

SWEEPS = 2
CHUNK = 8
GROUPS = 16
HALF = GROUPS // 2
LOCAL = (0, 1, 2, 3, 4, 7, 8)
ACROSS = (5, 6)
MESH = pl.DeviceIdType.MESH


def lane_moves(hop):
    row = lax.broadcasted_iota(jnp.int32, (256, 128), 0)
    lane = lax.broadcasted_iota(jnp.int32, (256, 128), 1)
    base, site = lane // 8 * 8, lane % 8
    low, plane = site // 4 == 0, site // 4 * 4
    across = base + (site + 4) % 8
    origin = (jnp.where(low, across, across + 128), jnp.where(low, across + 128, across),
              base + plane + (site + 1) % 4, base + plane + (site + 3) % 4)[hop]
    return jnp.where(row == origin, 1.0, 0.0).astype(jnp.bfloat16)


def swap_blocks(tiles):
    tiles = list(tiles)
    block = lax.broadcasted_iota(jnp.int32, tiles[0].shape, 1) // CHUNK
    for bit in (1, 2, 4, 8):
        high = block // bit % 2 == 1
        for i in range(GROUPS):
            if i & bit == 0:
                a, b = tiles[i], tiles[i | bit]
                tiles[i] = jnp.where(high, pltpu.roll(b, CHUNK * bit, 1), a)
                tiles[i | bit] = jnp.where(high, b, pltpu.roll(a, 128 - CHUNK * bit, 1))
    return tiles


def turned(alpha_re, alpha_im, v):
    re, im = v[:, :128], v[:, 128:]
    return jnp.concatenate([alpha_re * re - alpha_im * im, alpha_re * im + alpha_im * re], axis=1)


def kernel(n_grp, n_fold, counts, blocks, source, res_out, image_out, alphas,
           moves, raw, w_local, w_across, image, res, first_image, gath, last, edge_image, rims, local_rhs, red,
           load_sem, x_send, x_recv, r_send, r_recv, s_send, s_recv):
    bf16, f32 = jnp.bfloat16, jnp.float32
    rows, comps = blocks.shape[2], blocks.shape[3]
    nrhs = source.shape[1]
    total = n_grp * n_fold
    grp, fold = lax.axis_index("grp"), lax.axis_index("fold")
    me = grp * n_fold + fold
    loads = [pltpu.make_async_copy(blocks.at[m], raw.at[m], load_sem.at[m]) for m in range(9)]
    def device(index):
        return (lax.div(index, n_fold), lax.rem(index, n_fold))

    barrier = pltpu.get_barrier_semaphore()

    def greet(d, carry):
        pl.semaphore_signal(barrier, inc=1, device_id=device(lax.rem(me + d, total)), device_id_type=MESH)
        return carry

    lax.fori_loop(1, total, greet, 0, unroll=total <= 64)
    for load in loads:
        load.start()

    live = (counts[0] - 1).astype(f32)

    for p in range(2):
        planes = [source[p, k].astype(f32) for k in range(nrhs)]
        for t in range(0, rows, 8):
            tiles = [plane[t:t + 8] for plane in planes]
            tiles += [jnp.zeros((8, 128), f32)] * (GROUPS - nrhs)
            for g, tile in enumerate(swap_blocks(tiles)):
                res[g, t:t + 8, 128 * p:128 * p + 128] = tile * live if g >= HALF else tile

    pl.semaphore_wait(barrier, total - 1)

    def exchange(sweep, mine, slots, first_plane, last_plane):
        copies = []
        for side, src, step in ((0, first_plane, n_grp - 1), (1, last_plane, 1)):
            copies.append(pltpu.make_async_remote_copy(
                src_ref=src, dst_ref=rims.at[sweep, side, fold],
                send_sem=r_send.at[sweep, side, 0], recv_sem=r_recv.at[sweep, side, 0],
                device_id=(lax.rem(grp + step, n_grp), fold), device_id_type=MESH))
        for d in range(1, n_fold):
            copies.append(pltpu.make_async_remote_copy(
                src_ref=mine, dst_ref=slots.at[fold],
                send_sem=x_send.at[sweep, d], recv_sem=x_recv.at[sweep, d],
                device_id=(grp, lax.rem(fold + d, n_fold)), device_id_type=MESH))
        for copy in copies:
            copy.start()
        return copies

    def send_source():
        def fill(h, carry):
            lower, upper = res[h], res[h + HALF]
            gath[fold, h] = lower.astype(bf16)
            gath[fold, h + HALF] = upper.astype(bf16)
            last[h] = (upper * live + lower * (1.0 - live)).astype(bf16)
            return carry

        lax.fori_loop(0, HALF, fill, 0, unroll=2)
        return exchange(0, gath.at[fold], gath, gath.at[fold, pl.ds(0, HALF)], last)

    def send_image():
        return exchange(1, first_image.at[fold], first_image, edge_image.at[0], edge_image.at[1])

    def wait_gather(sweep, slots):
        for d in range(1, n_fold):
            slot = slots.at[lax.rem(fold + n_fold - d, n_fold)]
            pltpu.make_async_remote_copy(
                src_ref=slot, dst_ref=slot, send_sem=x_send.at[sweep, d], recv_sem=x_recv.at[sweep, d],
                device_id=(grp, lax.rem(fold + d, n_fold)), device_id_type=MESH).wait_recv()

    def forward(sweep, side, d, sender):
        slot = rims.at[sweep, side, sender]
        return pltpu.make_async_remote_copy(
            src_ref=slot, dst_ref=slot, send_sem=r_send.at[sweep, side, d],
            recv_sem=r_recv.at[sweep, side, d],
            device_id=(grp, lax.rem(fold + d, n_fold)), device_id_type=MESH)

    def pass_edge(sweep, side, edges):
        edges[side].wait_recv()
        passed = [forward(sweep, side, d, fold) for d in range(1, n_fold)]
        for copy in passed:
            copy.start()
        return passed

    def local_and_pass(sweep, edges):
        apply_local(0, 8)
        passed = pass_edge(sweep, 0, edges)
        apply_local(8, 12)
        passed += pass_edge(sweep, 1, edges)
        apply_local(12, 16)
        wait_edges(sweep)
        return passed

    def wait_edges(sweep):
        for side in range(2):
            for d in range(1, n_fold):
                forward(sweep, side, d, lax.rem(fold + n_fold - d, n_fold)).wait_recv()

    def whole_rows(read):
        parts = [read(f) for f in range(n_fold)]
        if rows % 16:
            return jnp.concatenate([part.astype(f32) for part in parts], axis=0).astype(bf16)
        return jnp.concatenate(parts, axis=0)

    def doubled(re, im):
        return jnp.concatenate(
            [jnp.concatenate([re, im], axis=1), jnp.concatenate([-im, re], axis=1)], axis=0)

    def stepped(alpha, start, moved):
        parts = [start(f).astype(f32) - turned(*alpha, moved(f).astype(f32)) for f in range(n_fold)]
        return jnp.concatenate(parts, axis=0).astype(bf16)

    def build_local(alpha):
        def pair(h, carry):
            if alpha is None:
                chunks = [whole_rows(lambda f, i=i: gath[f, 2 * h + i]) for i in range(2)]
            else:
                chunks = []
                for g in (2 * h, 2 * h + 1):
                    res[g] = res[g] - turned(*alpha, first_image[fold, g])
                    chunks.append(stepped(alpha, lambda f, g=g: gath[f, g], lambda f, g=g: first_image[f, g]))
            (are, aim), (bre, bim) = [(c[:, :128], c[:, 128:]) for c in chunks]
            local_rhs[0, 2 * h] = doubled(are, aim)
            local_rhs[0, 2 * h + 1] = doubled(bre, bim)
            left = jnp.concatenate([jnp.concatenate([are, aim, bre, bim], axis=0),
                                    jnp.concatenate([bre, bim, are, aim], axis=0)], axis=1)
            moved = jnp.dot(left, moves[...], preferred_element_type=f32).astype(bf16)
            for i in range(2):
                for hop in range(4):
                    cut = moved[2 * comps * i:2 * comps * (i + 1), 128 * hop:128 * hop + 128]
                    local_rhs[1 + hop, 2 * h + i] = doubled(cut[:comps], cut[comps:])
            return carry

        lax.fori_loop(0, HALF, pair, 0, unroll=2)

    row_site = lax.broadcasted_iota(jnp.int32, (8, 256), 0)
    lane_site = lax.broadcasted_iota(jnp.int32, (8, 256), 1) % CHUNK
    upper = {bit: row_site // bit % 2 == 1 for bit in (4, 2, 1)}
    stays = {bit: row_site // bit % 2 == lane_site // bit % 2 for bit in (4, 2, 1)}

    def same_site(product):
        out = []
        for t in range(0, rows, 8):
            parts = [product[CHUNK * (t + r):CHUNK * (t + r + 1)] for r in range(8)]
            for bit in (4, 2, 1):
                merged = []
                for a, b in zip(parts[:bit], parts[bit:]):
                    here = jnp.where(upper[bit], b, a)
                    there = pltpu.roll(jnp.where(upper[bit], a, b), 4 if bit == 4 else bit, 0)
                    if bit != 4:
                        there = jnp.where(upper[bit], there, pltpu.roll(jnp.where(upper[bit], a, b), 8 - bit, 0))
                    merged.append(jnp.where(stays[bit], here, there))
                parts = merged
            out.append(parts[0])
        return out[0] if len(out) == 1 else jnp.concatenate(out, axis=0)

    def apply_local(begin, end):
        def chunk(g, carry):
            plane, x, low = g // HALF * HALF, g % HALF // 2, g % 2
            ahead, behind = plane + (x + 1) % 4 * 2 + low, plane + (x + 3) % 4 * 2 + low
            rhs = jnp.concatenate(
                [local_rhs[0, g], local_rhs[0, ahead], local_rhs[0, behind]]
                + [local_rhs[1 + hop, g] for hop in range(4)], axis=0)
            image[g] = same_site(jnp.dot(w_local[g], rhs, preferred_element_type=f32))
            return carry

        lax.fori_loop(begin, end, chunk, 0, unroll=end - begin)

    def dots(a, r):
        are, aim, rre, rim = a[:, :128], a[:, 128:], r[:, :128], r[:, 128:]
        return are * rre + aim * rim, are * rim - aim * rre, are * are + aim * aim

    def apply_across(alpha):
        def plane_chunk(h, sums):
            if alpha is None:
                after, before = [whole_rows(lambda f, side=side: rims[0, side, f, h]) for side in range(2)]
            else:
                after, before = [stepped(alpha, lambda f, side=side: rims[0, side, f, h],
                                         lambda f, side=side: rims[1, side, f, h]) for side in range(2)]
            after = doubled(after[:, :128], after[:, 128:])
            before = doubled(before[:, :128], before[:, 128:])
            inner, outer = local_rhs[0, h], local_rhs[0, h + HALF]
            up = (outer.astype(f32) * live + after.astype(f32) * (1.0 - live)).astype(bf16)
            first = same_site(jnp.dot(w_across[h], jnp.concatenate([up, before], axis=0),
                                      preferred_element_type=f32))
            second = same_site(jnp.dot(w_across[h + HALF], jnp.concatenate([after, inner], axis=0),
                                       preferred_element_type=f32))
            first = first + image[h]
            second = (second + image[h + HALF]) * live
            if alpha is None:
                first_image[fold, h] = first
                first_image[fold, h + HALF] = second
                edge_image[0, h] = first.astype(bf16)
                edge_image[1, h] = (second + first * (1.0 - live)).astype(bf16)
            else:
                image[h] = first
                image[h + HALF] = second
            one, two = dots(first, res[h]), dots(second, res[h + HALF])
            return tuple(s + a + b for s, a, b in zip(sums, one, two))

        zero = jnp.zeros((rows, 128), f32)
        return lax.fori_loop(0, HALF, plane_chunk, (zero, zero, zero), unroll=4)

    row8 = lax.broadcasted_iota(jnp.int32, (8, 128), 0)
    lane8 = lax.broadcasted_iota(jnp.int32, (8, 128), 1)

    def spread(value):
        for step in (4, 2, 1):
            value = value + jnp.where(lane8 // step % 2 == 0,
                                      pltpu.roll(value, 128 - step, 1), pltpu.roll(value, step, 1))
        return value

    def send_sums(sweep, sums):
        re, im, norm = [jnp.sum(s, axis=0, keepdims=True) for s in sums]
        value = spread(jnp.where(row8 == 0, re, jnp.where(row8 == 1, im, norm)))
        spot = lane8[:1] % CHUNK
        red[sweep, 0] = jnp.where(spot == 0, value[0:1], jnp.where(spot == 1, value[1:2], value[2:3]))

        def send(d, carry):
            pltpu.make_async_remote_copy(
                src_ref=red.at[sweep, 0], dst_ref=red.at[sweep, d],
                send_sem=s_send.at[sweep], recv_sem=s_recv.at[sweep],
                device_id=device(lax.rem(me + d, total)), device_id_type=MESH).start()
            return carry

        lax.fori_loop(1, total, send, 0, unroll=total <= 64)

    def wait_sums(sweep):
        everyone = red.at[sweep, pl.ds(1, total - 1)]
        pltpu.make_async_copy(everyone, everyone, s_recv.at[sweep]).wait()
        value = jnp.broadcast_to(jnp.sum(red[sweep], axis=0), (8, 128))
        value = spread(jnp.where(lane8 % CHUNK == row8, value, 0.0))
        norm = jnp.where(lane8[:1] < CHUNK * nrhs, value[2:3], 1.0)
        return value[0:1] / norm, value[1:2] / norm

    def natural(held, out):
        for p in range(2):
            for t in range(0, rows, 8):
                tiles = swap_blocks([held[g, t:t + 8, 128 * p:128 * p + 128] for g in range(GROUPS)])
                for k in range(nrhs):
                    out[p, k, t:t + 8] = tiles[k]

    copies = send_source()
    for hop in range(4):
        moves[:, 128 * hop:128 * hop + 128] = lane_moves(hop)
    for m in range(9):
        loads[m].wait()
        place = LOCAL.index(m) if m in LOCAL else ACROSS.index(m)
        target = w_local if m in LOCAL else w_across

        def two_rows(i, carry, m=m, place=place, target=target):
            flipped = []
            for a in range(2):
                both = jnp.concatenate([raw[m, 0, 2 * i + a], raw[m, 1, 2 * i + a]], axis=0)
                flipped.append(both.T.astype(f32))
            for g in range(GROUPS):
                piece = jnp.concatenate([f[8 * g:8 * g + 8] for f in flipped], axis=0)
                target[g, pl.ds(pl.multiple_of(16 * i, 16), 16),
                       2 * comps * place:2 * comps * (place + 1)] = piece.astype(bf16)
            return carry

        lax.fori_loop(0, rows // 2, two_rows, 0, unroll=min(rows // 2, 8))
    wait_gather(0, gath)
    build_local(None)
    copies += local_and_pass(0, copies[:2])
    send_sums(0, apply_across(None))
    later = send_image()
    first = wait_sums(0)
    wait_gather(1, first_image)
    build_local(first)
    later += local_and_pass(1, later[:2])
    send_sums(1, apply_across(first))
    natural(res, res_out)
    natural(image, image_out)
    second = wait_sums(1)
    alphas[...] = jnp.where(row8 == 0, first[0], jnp.where(row8 == 1, first[1], jnp.where(
        row8 == 2, second[0], jnp.where(row8 == 3, second[1], jnp.where(lane8 < 64, 1.0, live)))))
    for copy in copies + later:
        copy.wait_send()
    for sweep in range(SWEEPS):
        everyone = red.at[sweep, pl.ds(1, total - 1)]
        pltpu.make_async_copy(everyone, everyone, s_send.at[sweep]).wait()


def finish(source, res, image, alphas, sol_out, res_out):
    nrhs, rows = source.shape[1:3]
    f32 = jnp.float32
    kept = jnp.broadcast_to(alphas[4:5], (rows, 128))
    for k in range(nrhs):
        are, aim, bre, bim = [jnp.broadcast_to(alphas[i:i + 1, CHUNK * k:CHUNK * k + 1], (rows, 128))
                              for i in range(4)]
        sre, sim = [source[p, k].astype(f32) * kept for p in range(2)]
        rre, rim, ire, iim = res[0, k], res[1, k], image[0, k], image[1, k]
        sol_out[0, k] = (are * sre - aim * sim) + (bre * rre - bim * rim)
        sol_out[1, k] = (are * sim + aim * sre) + (bre * rim + bim * rre)
        res_out[0, k] = rre - (bre * ire - bim * iim)
        res_out[1, k] = rim - (bre * iim + bim * ire)


def body(n_grp, n_fold, blocks, source, plane_counts):
    rows, comps = blocks.shape[2], blocks.shape[3]
    nrhs = source.shape[2]
    bf16, f32 = jnp.bfloat16, jnp.float32
    shape = (2, nrhs, rows, GROUPS * CHUNK)
    vmem = pl.BlockSpec(memory_space=pltpu.VMEM)
    total = n_grp * n_fold
    held = jax.ShapeDtypeStruct(shape, f32)
    smem = pl.BlockSpec(memory_space=pltpu.SMEM)
    source = source.transpose(0, 2, 1, 3)
    iterate = pl.pallas_call(
        functools.partial(kernel, n_grp, n_fold),
        out_shape=(held, held, jax.ShapeDtypeStruct((8, 128), f32)),
        in_specs=[smem, pl.BlockSpec(memory_space=pl.ANY), vmem],
        out_specs=(vmem, vmem, vmem),
        scratch_shapes=[
            pltpu.VMEM((256, 512), bf16),
            pltpu.VMEM(blocks.shape, bf16),
            pltpu.VMEM((GROUPS, rows * CHUNK, len(LOCAL) * 2 * comps), bf16),
            pltpu.VMEM((GROUPS, rows * CHUNK, len(ACROSS) * 2 * comps), bf16),
            pltpu.VMEM((GROUPS, rows, 256), f32),
            pltpu.VMEM((GROUPS, rows, 256), f32),
            pltpu.VMEM((n_fold, GROUPS, rows, 256), f32),
            pltpu.VMEM((n_fold, GROUPS, rows, 256), bf16),
            pltpu.VMEM((HALF, rows, 256), bf16),
            pltpu.VMEM((2, HALF, rows, 256), bf16),
            pltpu.VMEM((SWEEPS, 2, n_fold, HALF, rows, 256), bf16),
            pltpu.VMEM((5, GROUPS, 2 * comps, 256), bf16),
            pltpu.VMEM((SWEEPS, total, 1, 128), f32),
            pltpu.SemaphoreType.DMA((9,)),
            pltpu.SemaphoreType.DMA((SWEEPS, n_fold)),
            pltpu.SemaphoreType.DMA((SWEEPS, n_fold)),
            pltpu.SemaphoreType.DMA((SWEEPS, 2, n_fold)),
            pltpu.SemaphoreType.DMA((SWEEPS, 2, n_fold)),
            pltpu.SemaphoreType.DMA((SWEEPS,)),
            pltpu.SemaphoreType.DMA((SWEEPS,)),
        ],
        compiler_params=pltpu.CompilerParams(
            collective_id=0, has_side_effects=True, vmem_limit_bytes=52 * 1024 * 1024),
    )(plane_counts, blocks, source)
    outs = pl.pallas_call(
        finish,
        out_shape=(jax.ShapeDtypeStruct(shape, f32), jax.ShapeDtypeStruct(shape, f32)),
        in_specs=[vmem] * 4,
        out_specs=(vmem, vmem),
        compiler_params=pltpu.CompilerParams(vmem_limit_bytes=8 * 1024 * 1024),
    )(source, *iterate)
    return tuple(out.transpose(0, 2, 1, 3) for out in outs)


def solution(mesh):
    return jax.shard_map(
        functools.partial(body, mesh.shape["grp"], mesh.shape["fold"]),
        mesh=mesh,
        in_specs=(P(None, None, "fold", None, "grp"), P(None, "fold", None, "grp"), P("grp")),
        out_specs=(P(None, "fold", None, "grp"), P(None, "fold", None, "grp")),
        check_vma=False,
    )
```

```python
import functools

import jax
import jax.numpy as jnp
import numpy as np
from jax import lax
from jax.experimental import pallas as pl
from jax.experimental.pallas import tpu as pltpu
from jax.sharding import PartitionSpec as P

SWEEPS = 2
CHUNK = 8
GROUPS = 16
HALF = GROUPS // 2
LOCAL = (0, 1, 2, 3, 4, 7, 8)
ACROSS = (5, 6)
MESH = pl.DeviceIdType.MESH


def lane_moves(hop):
    row = lax.broadcasted_iota(jnp.int32, (256, 128), 0)
    lane = lax.broadcasted_iota(jnp.int32, (256, 128), 1)
    base, site = lane // 8 * 8, lane % 8
    low, plane = site // 4 == 0, site // 4 * 4
    across = base + (site + 4) % 8
    origin = (jnp.where(low, across, across + 128), jnp.where(low, across + 128, across),
              base + plane + (site + 1) % 4, base + plane + (site + 3) % 4)[hop]
    return jnp.where(row == origin, 1.0, 0.0).astype(jnp.bfloat16)


def swap_blocks(tiles):
    tiles = list(tiles)
    block = lax.broadcasted_iota(jnp.int32, tiles[0].shape, 1) // CHUNK
    for bit in (1, 2, 4, 8):
        high = block // bit % 2 == 1
        for i in range(GROUPS):
            if i & bit == 0:
                a, b = tiles[i], tiles[i | bit]
                tiles[i] = jnp.where(high, pltpu.roll(b, CHUNK * bit, 1), a)
                tiles[i | bit] = jnp.where(high, b, pltpu.roll(a, 128 - CHUNK * bit, 1))
    return tiles


def pack(chunks):
    halves = [chunk[:, 128 * p:128 * p + 128] for chunk in chunks for p in range(2)]
    lane = lax.broadcasted_iota(jnp.int32, halves[0].shape, 1)
    return [jnp.where(lane < 96, halves[j], pltpu.roll(halves[6 + j // 3], 96 - 32 * (j % 3), 1)) for j in range(6)]


def unpack(tiles):
    lane = lax.broadcasted_iota(jnp.int32, tiles[0].shape, 1)
    halves = [jnp.where(lane < 96, tile, 0.0) for tile in tiles]
    for a, b, c in (tiles[:3], tiles[3:]):
        halves.append(jnp.where(lane < 32, pltpu.roll(a, 32, 1), jnp.where(
            lane < 64, pltpu.roll(b, 64, 1), jnp.where(lane < 96, pltpu.roll(c, 96, 1), 0.0))))
    return [jnp.concatenate(halves[2 * i:2 * i + 2], axis=1) for i in range(4)]


def turned(alpha_re, alpha_im, v):
    re, im = v[:, :128], v[:, 128:]
    return jnp.concatenate([alpha_re * re - alpha_im * im, alpha_re * im + alpha_im * re], axis=1)


def kernel(n_grp, n_fold, counts, blocks, source, res_out, image_out, alphas,
           moves, raw, w_local, w_across, image, res, first_image, gath, edge_pack, rims, local_rhs, red,
           load_sem, x_send, x_recv, r_send, r_recv, s_send, s_recv):
    bf16, f32 = jnp.bfloat16, jnp.float32
    rows, comps = blocks.shape[2], blocks.shape[3]
    nrhs = source.shape[1]
    total = n_grp * n_fold
    grp, fold = lax.axis_index("grp"), lax.axis_index("fold")
    me = grp * n_fold + fold
    loads = [pltpu.make_async_copy(blocks.at[m], raw.at[m], load_sem.at[m]) for m in range(9)]
    def device(index):
        return (lax.div(index, n_fold), lax.rem(index, n_fold))

    barrier = pltpu.get_barrier_semaphore()

    def greet(d, carry):
        pl.semaphore_signal(barrier, inc=1, device_id=device(lax.rem(me + d, total)), device_id_type=MESH)
        return carry

    lax.fori_loop(1, total, greet, 0, unroll=total <= 64)
    for load in loads:
        load.start()

    live = (counts[0] - 1).astype(f32)

    for p in range(2):
        planes = [source[p, k].astype(f32) for k in range(nrhs)]
        for t in range(0, rows, 8):
            tiles = [plane[t:t + 8] for plane in planes]
            tiles += [jnp.zeros((8, 128), f32)] * (GROUPS - nrhs)
            for g, tile in enumerate(swap_blocks(tiles)):
                res[g, t:t + 8, 128 * p:128 * p + 128] = tile * live if g >= HALF else tile

    pl.semaphore_wait(barrier, total - 1)

    def send_edges(sweep, held):
        def group(q, carry):
            lower = [held(4 * q + i) for i in range(4)]
            upper = [held(4 * q + i + HALF) for i in range(4)]
            final = [b + a * (1.0 - live) for a, b in zip(lower, upper)]
            for side, chunks in enumerate((lower, final)):
                for j, tile in enumerate(pack(chunks)):
                    edge_pack[sweep, side, q, j] = tile.astype(bf16)
            return carry

        lax.fori_loop(0, 2, group, 0, unroll=2)
        copies = [pltpu.make_async_remote_copy(
            src_ref=edge_pack.at[sweep, side], dst_ref=rims.at[sweep, side, fold],
            send_sem=r_send.at[sweep, side, 0], recv_sem=r_recv.at[sweep, side, 0],
            device_id=(lax.rem(grp + step, n_grp), fold), device_id_type=MESH)
            for side, step in ((0, n_grp - 1), (1, 1))]
        for copy in copies:
            copy.start()
        return copies

    def send_gather(sweep, slots):
        copies = [pltpu.make_async_remote_copy(
            src_ref=slots.at[fold], dst_ref=slots.at[fold],
            send_sem=x_send.at[sweep, d], recv_sem=x_recv.at[sweep, d],
            device_id=(grp, lax.rem(fold + d, n_fold)), device_id_type=MESH) for d in range(1, n_fold)]
        for copy in copies:
            copy.start()
        return copies

    def send_source():
        edges = send_edges(0, lambda g: res[g])

        def fill(h, carry):
            gath[fold, h] = res[h].astype(bf16)
            return carry

        lax.fori_loop(0, GROUPS, fill, 0, unroll=4)
        return edges + send_gather(0, gath)

    def send_image():
        return send_edges(1, lambda g: first_image[fold, g]) + send_gather(1, first_image)

    def wait_gather(sweep, slots):
        for d in range(1, n_fold):
            slot = slots.at[lax.rem(fold + n_fold - d, n_fold)]
            pltpu.make_async_remote_copy(
                src_ref=slot, dst_ref=slot, send_sem=x_send.at[sweep, d], recv_sem=x_recv.at[sweep, d],
                device_id=(grp, lax.rem(fold + d, n_fold)), device_id_type=MESH).wait_recv()

    def forward(sweep, side, d, sender):
        slot = rims.at[sweep, side, sender]
        return pltpu.make_async_remote_copy(
            src_ref=slot, dst_ref=slot, send_sem=r_send.at[sweep, side, d],
            recv_sem=r_recv.at[sweep, side, d],
            device_id=(grp, lax.rem(fold + d, n_fold)), device_id_type=MESH)

    def pass_edge(sweep, side, edges):
        edges[side].wait_recv()
        passed = [forward(sweep, side, d, fold) for d in range(1, n_fold)]
        for copy in passed:
            copy.start()
        return passed

    def local_and_pass(sweep, edges):
        apply_local(0, 6)
        passed = pass_edge(sweep, 0, edges)
        apply_local(6, 10)
        passed += pass_edge(sweep, 1, edges)
        apply_local(10, 16)
        wait_edges(sweep)
        return passed

    def wait_edges(sweep):
        for side in range(2):
            for d in range(1, n_fold):
                forward(sweep, side, d, lax.rem(fold + n_fold - d, n_fold)).wait_recv()

    def whole_rows(read):
        parts = [read(f) for f in range(n_fold)]
        if rows % 16:
            return jnp.concatenate([part.astype(f32) for part in parts], axis=0).astype(bf16)
        return jnp.concatenate(parts, axis=0)

    def doubled(re, im):
        return jnp.concatenate(
            [jnp.concatenate([re, im], axis=1), jnp.concatenate([-im, re], axis=1)], axis=0)

    def stepped(alpha, start, moved):
        parts = [start(f).astype(f32) - turned(*alpha, moved(f).astype(f32)) for f in range(n_fold)]
        return jnp.concatenate(parts, axis=0).astype(bf16)

    def edge_chunks(alpha, side, q):
        folds = []
        for f in range(n_fold):
            start, moved = [unpack([rims[sweep, side, f, q, j].astype(f32) for j in range(6)])
                            if sweep == 0 or alpha is not None else None for sweep in range(2)]
            folds.append(start if alpha is None else [a - turned(*alpha, b) for a, b in zip(start, moved)])
        return [jnp.concatenate(parts, axis=0).astype(bf16) for parts in zip(*folds)]

    def build_local(alpha):
        def pair(h, carry):
            if alpha is None:
                chunks = [whole_rows(lambda f, i=i: gath[f, 2 * h + i]) for i in range(2)]
            else:
                chunks = []
                for g in (2 * h, 2 * h + 1):
                    res[g] = res[g] - turned(*alpha, first_image[fold, g])
                    chunks.append(stepped(alpha, lambda f, g=g: gath[f, g], lambda f, g=g: first_image[f, g]))
            (are, aim), (bre, bim) = [(c[:, :128], c[:, 128:]) for c in chunks]
            local_rhs[0, 2 * h] = doubled(are, aim)
            local_rhs[0, 2 * h + 1] = doubled(bre, bim)
            left = jnp.concatenate([jnp.concatenate([are, aim, bre, bim], axis=0),
                                    jnp.concatenate([bre, bim, are, aim], axis=0)], axis=1)
            moved = jnp.dot(left, moves[...], preferred_element_type=f32).astype(bf16)
            for i in range(2):
                for hop in range(4):
                    cut = moved[2 * comps * i:2 * comps * (i + 1), 128 * hop:128 * hop + 128]
                    local_rhs[1 + hop, 2 * h + i] = doubled(cut[:comps], cut[comps:])
            return carry

        lax.fori_loop(0, HALF, pair, 0, unroll=2)

    row_site = lax.broadcasted_iota(jnp.int32, (8, 256), 0)
    lane_site = lax.broadcasted_iota(jnp.int32, (8, 256), 1) % CHUNK
    upper = {bit: row_site // bit % 2 == 1 for bit in (4, 2, 1)}
    stays = {bit: row_site // bit % 2 == lane_site // bit % 2 for bit in (4, 2, 1)}

    def same_site(product):
        out = []
        for t in range(0, rows, 8):
            parts = [product[CHUNK * (t + r):CHUNK * (t + r + 1)] for r in range(8)]
            for bit in (4, 2, 1):
                merged = []
                for a, b in zip(parts[:bit], parts[bit:]):
                    here = jnp.where(upper[bit], b, a)
                    there = pltpu.roll(jnp.where(upper[bit], a, b), 4 if bit == 4 else bit, 0)
                    if bit != 4:
                        there = jnp.where(upper[bit], there, pltpu.roll(jnp.where(upper[bit], a, b), 8 - bit, 0))
                    merged.append(jnp.where(stays[bit], here, there))
                parts = merged
            out.append(parts[0])
        return out[0] if len(out) == 1 else jnp.concatenate(out, axis=0)

    def apply_local(begin, end):
        def chunk(g, carry):
            plane, x, low = g // HALF * HALF, g % HALF // 2, g % 2
            ahead, behind = plane + (x + 1) % 4 * 2 + low, plane + (x + 3) % 4 * 2 + low
            rhs = jnp.concatenate(
                [local_rhs[0, g], local_rhs[0, ahead], local_rhs[0, behind]]
                + [local_rhs[1 + hop, g] for hop in range(4)], axis=0)
            image[g] = same_site(jnp.dot(w_local[g], rhs, preferred_element_type=f32))
            return carry

        lax.fori_loop(begin, end, chunk, 0, unroll=end - begin)

    def dots(a, r):
        are, aim, rre, rim = a[:, :128], a[:, 128:], r[:, :128], r[:, 128:]
        return are * rre + aim * rim, are * rim - aim * rre, are * are + aim * aim

    def apply_across(alpha):
        def plane_chunk(h, after, before, sums):
            after = doubled(after[:, :128], after[:, 128:])
            before = doubled(before[:, :128], before[:, 128:])
            inner, outer = local_rhs[0, h], local_rhs[0, h + HALF]
            up = (outer.astype(f32) * live + after.astype(f32) * (1.0 - live)).astype(bf16)
            first = same_site(jnp.dot(w_across[h], jnp.concatenate([up, before], axis=0),
                                      preferred_element_type=f32))
            second = same_site(jnp.dot(w_across[h + HALF], jnp.concatenate([after, inner], axis=0),
                                       preferred_element_type=f32))
            first = first + image[h]
            second = (second + image[h + HALF]) * live
            if alpha is None:
                first_image[fold, h] = first
                first_image[fold, h + HALF] = second
            else:
                image[h] = first
                image[h + HALF] = second
            one, two = dots(first, res[h]), dots(second, res[h + HALF])
            return tuple(s + a + b for s, a, b in zip(sums, one, two))

        zero = jnp.zeros((rows, 128), f32)

        def group(q, sums):
            sides = [edge_chunks(alpha, side, q) for side in range(2)]
            for i in range(4):
                sums = plane_chunk(4 * q + i, sides[0][i], sides[1][i], sums)
            return sums

        return lax.fori_loop(0, 2, group, (zero, zero, zero))

    row8 = lax.broadcasted_iota(jnp.int32, (8, 128), 0)
    lane8 = lax.broadcasted_iota(jnp.int32, (8, 128), 1)

    def spread(value):
        for step in (4, 2, 1):
            value = value + jnp.where(lane8 // step % 2 == 0,
                                      pltpu.roll(value, 128 - step, 1), pltpu.roll(value, step, 1))
        return value

    def send_sums(sweep, sums):
        re, im, norm = [jnp.sum(s, axis=0, keepdims=True) for s in sums]
        value = spread(jnp.where(row8 == 0, re, jnp.where(row8 == 1, im, norm)))
        spot = lane8[:1] % CHUNK
        red[sweep, 0] = jnp.where(spot == 0, value[0:1], jnp.where(spot == 1, value[1:2], value[2:3]))

        def send(d, carry):
            pltpu.make_async_remote_copy(
                src_ref=red.at[sweep, 0], dst_ref=red.at[sweep, d],
                send_sem=s_send.at[sweep], recv_sem=s_recv.at[sweep],
                device_id=device(lax.rem(me + d, total)), device_id_type=MESH).start()
            return carry

        lax.fori_loop(1, total, send, 0, unroll=total <= 64)

    def wait_sums(sweep):
        everyone = red.at[sweep, pl.ds(1, total - 1)]
        pltpu.make_async_copy(everyone, everyone, s_recv.at[sweep]).wait()
        value = jnp.broadcast_to(jnp.sum(red[sweep], axis=0), (8, 128))
        value = spread(jnp.where(lane8 % CHUNK == row8, value, 0.0))
        norm = jnp.where(lane8[:1] < CHUNK * nrhs, value[2:3], 1.0)
        return value[0:1] / norm, value[1:2] / norm

    def natural(held, out):
        for p in range(2):
            for t in range(0, rows, 8):
                tiles = swap_blocks([held[g, t:t + 8, 128 * p:128 * p + 128] for g in range(GROUPS)])
                for k in range(nrhs):
                    out[p, k, t:t + 8] = tiles[k]

    copies = send_source()
    for hop in range(4):
        moves[:, 128 * hop:128 * hop + 128] = lane_moves(hop)
    for m in range(9):
        loads[m].wait()
        place = LOCAL.index(m) if m in LOCAL else ACROSS.index(m)
        target = w_local if m in LOCAL else w_across

        def two_rows(i, carry, m=m, place=place, target=target):
            flipped = []
            for a in range(2):
                both = jnp.concatenate([raw[m, 0, 2 * i + a], raw[m, 1, 2 * i + a]], axis=0)
                flipped.append(both.T.astype(f32))
            for g in range(GROUPS):
                piece = jnp.concatenate([f[8 * g:8 * g + 8] for f in flipped], axis=0)
                target[g, pl.ds(pl.multiple_of(16 * i, 16), 16),
                       2 * comps * place:2 * comps * (place + 1)] = piece.astype(bf16)
            return carry

        lax.fori_loop(0, rows // 2, two_rows, 0, unroll=min(rows // 2, 8))
    wait_gather(0, gath)
    build_local(None)
    copies += local_and_pass(0, copies[:2])
    send_sums(0, apply_across(None))
    later = send_image()
    first = wait_sums(0)
    wait_gather(1, first_image)
    build_local(first)
    later += local_and_pass(1, later[:2])
    send_sums(1, apply_across(first))
    natural(res, res_out)
    natural(image, image_out)
    second = wait_sums(1)
    alphas[...] = jnp.where(row8 == 0, first[0], jnp.where(row8 == 1, first[1], jnp.where(
        row8 == 2, second[0], jnp.where(row8 == 3, second[1], jnp.where(lane8 < 64, 1.0, live)))))
    for copy in copies + later:
        copy.wait_send()
    for sweep in range(SWEEPS):
        everyone = red.at[sweep, pl.ds(1, total - 1)]
        pltpu.make_async_copy(everyone, everyone, s_send.at[sweep]).wait()


def finish(source, res, image, alphas, sol_out, res_out):
    nrhs, rows = source.shape[1:3]
    f32 = jnp.float32
    kept = jnp.broadcast_to(alphas[4:5], (rows, 128))
    for k in range(nrhs):
        are, aim, bre, bim = [jnp.broadcast_to(alphas[i:i + 1, CHUNK * k:CHUNK * k + 1], (rows, 128))
                              for i in range(4)]
        sre, sim = [source[p, k].astype(f32) * kept for p in range(2)]
        rre, rim, ire, iim = res[0, k], res[1, k], image[0, k], image[1, k]
        sol_out[0, k] = (are * sre - aim * sim) + (bre * rre - bim * rim)
        sol_out[1, k] = (are * sim + aim * sre) + (bre * rim + bim * rre)
        res_out[0, k] = rre - (bre * ire - bim * iim)
        res_out[1, k] = rim - (bre * iim + bim * ire)


def body(n_grp, n_fold, blocks, source, plane_counts):
    rows, comps = blocks.shape[2], blocks.shape[3]
    nrhs = source.shape[2]
    bf16, f32 = jnp.bfloat16, jnp.float32
    shape = (2, nrhs, rows, GROUPS * CHUNK)
    vmem = pl.BlockSpec(memory_space=pltpu.VMEM)
    total = n_grp * n_fold
    held = jax.ShapeDtypeStruct(shape, f32)
    smem = pl.BlockSpec(memory_space=pltpu.SMEM)
    source = source.transpose(0, 2, 1, 3)
    iterate = pl.pallas_call(
        functools.partial(kernel, n_grp, n_fold),
        out_shape=(held, held, jax.ShapeDtypeStruct((8, 128), f32)),
        in_specs=[smem, pl.BlockSpec(memory_space=pl.ANY), vmem],
        out_specs=(vmem, vmem, vmem),
        scratch_shapes=[
            pltpu.VMEM((256, 512), bf16),
            pltpu.VMEM(blocks.shape, bf16),
            pltpu.VMEM((GROUPS, rows * CHUNK, len(LOCAL) * 2 * comps), bf16),
            pltpu.VMEM((GROUPS, rows * CHUNK, len(ACROSS) * 2 * comps), bf16),
            pltpu.VMEM((GROUPS, rows, 256), f32),
            pltpu.VMEM((GROUPS, rows, 256), f32),
            pltpu.VMEM((n_fold, GROUPS, rows, 256), f32),
            pltpu.VMEM((n_fold, GROUPS, rows, 256), bf16),
            pltpu.VMEM((SWEEPS, 2, 2, 6, rows, 128), bf16),
            pltpu.VMEM((SWEEPS, 2, n_fold, 2, 6, rows, 128), bf16),
            pltpu.VMEM((5, GROUPS, 2 * comps, 256), bf16),
            pltpu.VMEM((SWEEPS, total, 1, 128), f32),
            pltpu.SemaphoreType.DMA((9,)),
            pltpu.SemaphoreType.DMA((SWEEPS, n_fold)),
            pltpu.SemaphoreType.DMA((SWEEPS, n_fold)),
            pltpu.SemaphoreType.DMA((SWEEPS, 2, n_fold)),
            pltpu.SemaphoreType.DMA((SWEEPS, 2, n_fold)),
            pltpu.SemaphoreType.DMA((SWEEPS,)),
            pltpu.SemaphoreType.DMA((SWEEPS,)),
        ],
        compiler_params=pltpu.CompilerParams(
            collective_id=0, has_side_effects=True, vmem_limit_bytes=52 * 1024 * 1024),
    )(plane_counts, blocks, source)
    outs = pl.pallas_call(
        finish,
        out_shape=(jax.ShapeDtypeStruct(shape, f32), jax.ShapeDtypeStruct(shape, f32)),
        in_specs=[vmem] * 4,
        out_specs=(vmem, vmem),
        compiler_params=pltpu.CompilerParams(vmem_limit_bytes=8 * 1024 * 1024),
    )(source, *iterate)
    return tuple(out.transpose(0, 2, 1, 3) for out in outs)


def solution(mesh):
    return jax.shard_map(
        functools.partial(body, mesh.shape["grp"], mesh.shape["fold"]),
        mesh=mesh,
        in_specs=(P(None, None, "fold", None, "grp"), P(None, "fold", None, "grp"), P("grp")),
        out_specs=(P(None, "fold", None, "grp"), P(None, "fold", None, "grp")),
        check_vma=False,
    )
```

```python
import functools

import jax
import jax.numpy as jnp
import numpy as np
from jax import lax
from jax.experimental import pallas as pl
from jax.experimental.pallas import tpu as pltpu
from jax.sharding import PartitionSpec as P

SWEEPS = 2
CHUNK = 8
GROUPS = 16
HALF = GROUPS // 2
LOCAL = (0, 1, 2, 3, 4, 7, 8)
ACROSS = (5, 6)
MESH = pl.DeviceIdType.MESH


def lane_moves(hop):
    row = lax.broadcasted_iota(jnp.int32, (256, 128), 0)
    lane = lax.broadcasted_iota(jnp.int32, (256, 128), 1)
    base, site = lane // 8 * 8, lane % 8
    low, plane = site // 4 == 0, site // 4 * 4
    across = base + (site + 4) % 8
    origin = (jnp.where(low, across, across + 128), jnp.where(low, across + 128, across),
              base + plane + (site + 1) % 4, base + plane + (site + 3) % 4)[hop]
    return jnp.where(row == origin, 1.0, 0.0).astype(jnp.bfloat16)


def swap_blocks(tiles):
    tiles = list(tiles)
    block = lax.broadcasted_iota(jnp.int32, tiles[0].shape, 1) // CHUNK
    for bit in (1, 2, 4, 8):
        high = block // bit % 2 == 1
        for i in range(GROUPS):
            if i & bit == 0:
                a, b = tiles[i], tiles[i | bit]
                tiles[i] = jnp.where(high, pltpu.roll(b, CHUNK * bit, 1), a)
                tiles[i | bit] = jnp.where(high, b, pltpu.roll(a, 128 - CHUNK * bit, 1))
    return tiles


def pack(chunks):
    halves = [chunk[:, 128 * p:128 * p + 128] for chunk in chunks for p in range(2)]
    lane = lax.broadcasted_iota(jnp.int32, halves[0].shape, 1)
    return [jnp.where(lane < 96, halves[j], pltpu.roll(halves[6 + j // 3], 96 - 32 * (j % 3), 1)) for j in range(6)]


def unpack(tiles):
    lane = lax.broadcasted_iota(jnp.int32, tiles[0].shape, 1)
    halves = [jnp.where(lane < 96, tile, 0.0) for tile in tiles]
    for a, b, c in (tiles[:3], tiles[3:]):
        halves.append(jnp.where(lane < 32, pltpu.roll(a, 32, 1), jnp.where(
            lane < 64, pltpu.roll(b, 64, 1), jnp.where(lane < 96, pltpu.roll(c, 96, 1), 0.0))))
    return [jnp.concatenate(halves[2 * i:2 * i + 2], axis=1) for i in range(4)]


def turned(alpha_re, alpha_im, v):
    re, im = v[:, :128], v[:, 128:]
    return jnp.concatenate([alpha_re * re - alpha_im * im, alpha_re * im + alpha_im * re], axis=1)


def kernel(n_grp, n_fold, counts, blocks, source_hbm, res_out, image_out, alphas,
           source, moves, raw, w_local, w_across, image, res, first_image, gath, edge_pack, rims, local_rhs, red,
           source_sem, load_sem, x_send, x_recv, r_send, r_recv, s_send, s_recv):
    bf16, f32 = jnp.bfloat16, jnp.float32
    rows, comps = blocks.shape[2], blocks.shape[3]
    nrhs = source_hbm.shape[1]
    total = n_grp * n_fold
    grp, fold = lax.axis_index("grp"), lax.axis_index("fold")
    me = grp * n_fold + fold
    fetch = pltpu.make_async_copy(source_hbm, source, source_sem)
    fetch.start()
    loads = [pltpu.make_async_copy(blocks.at[m], raw.at[m], load_sem.at[m]) for m in range(9)]
    def device(index):
        return (lax.div(index, n_fold), lax.rem(index, n_fold))

    barrier = pltpu.get_barrier_semaphore()

    def greet(d, carry):
        pl.semaphore_signal(barrier, inc=1, device_id=device(lax.rem(me + d, total)), device_id_type=MESH)
        return carry

    lax.fori_loop(1, total, greet, 0, unroll=total <= 64)
    for load in loads:
        load.start()

    live = (counts[0] - 1).astype(f32)
    fetch.wait()

    for p in range(2):
        planes = [source[p, k].astype(f32) for k in range(nrhs)]
        for t in range(0, rows, 8):
            tiles = [plane[t:t + 8] for plane in planes]
            tiles += [jnp.zeros((8, 128), f32)] * (GROUPS - nrhs)
            for g, tile in enumerate(swap_blocks(tiles)):
                res[g, t:t + 8, 128 * p:128 * p + 128] = tile * live if g >= HALF else tile

    pl.semaphore_wait(barrier, total - 1)

    def send_edges(sweep, held):
        def group(q, carry):
            lower = [held(4 * q + i) for i in range(4)]
            upper = [held(4 * q + i + HALF) for i in range(4)]
            final = [b + a * (1.0 - live) for a, b in zip(lower, upper)]
            for side, chunks in enumerate((lower, final)):
                for j, tile in enumerate(pack(chunks)):
                    edge_pack[sweep, side, q, j] = tile.astype(bf16)
            return carry

        lax.fori_loop(0, 2, group, 0, unroll=2)
        copies = [pltpu.make_async_remote_copy(
            src_ref=edge_pack.at[sweep, side], dst_ref=rims.at[sweep, side, fold],
            send_sem=r_send.at[sweep, side, 0], recv_sem=r_recv.at[sweep, side, 0],
            device_id=(lax.rem(grp + step, n_grp), fold), device_id_type=MESH)
            for side, step in ((0, n_grp - 1), (1, 1))]
        for copy in copies:
            copy.start()
        return copies

    def send_gather(sweep, slots):
        copies = [pltpu.make_async_remote_copy(
            src_ref=slots.at[fold], dst_ref=slots.at[fold],
            send_sem=x_send.at[sweep, d], recv_sem=x_recv.at[sweep, d],
            device_id=(grp, lax.rem(fold + d, n_fold)), device_id_type=MESH) for d in range(1, n_fold)]
        for copy in copies:
            copy.start()
        return copies

    def send_source():
        edges = send_edges(0, lambda g: res[g])

        def fill(h, carry):
            gath[fold, h] = res[h].astype(bf16)
            return carry

        lax.fori_loop(0, GROUPS, fill, 0, unroll=4)
        return edges + send_gather(0, gath)

    def send_image():
        return send_edges(1, lambda g: first_image[fold, g]) + send_gather(1, first_image)

    def wait_gather(sweep, slots):
        for d in range(1, n_fold):
            slot = slots.at[lax.rem(fold + n_fold - d, n_fold)]
            pltpu.make_async_remote_copy(
                src_ref=slot, dst_ref=slot, send_sem=x_send.at[sweep, d], recv_sem=x_recv.at[sweep, d],
                device_id=(grp, lax.rem(fold + d, n_fold)), device_id_type=MESH).wait_recv()

    def forward(sweep, side, d, sender):
        slot = rims.at[sweep, side, sender]
        return pltpu.make_async_remote_copy(
            src_ref=slot, dst_ref=slot, send_sem=r_send.at[sweep, side, d],
            recv_sem=r_recv.at[sweep, side, d],
            device_id=(grp, lax.rem(fold + d, n_fold)), device_id_type=MESH)

    def pass_edge(sweep, side, edges):
        edges[side].wait_recv()
        passed = [forward(sweep, side, d, fold) for d in range(1, n_fold)]
        for copy in passed:
            copy.start()
        return passed

    def local_and_pass(sweep, edges):
        apply_local(0, 6)
        passed = pass_edge(sweep, 0, edges)
        apply_local(6, 10)
        passed += pass_edge(sweep, 1, edges)
        apply_local(10, 16)
        wait_edges(sweep)
        return passed

    def wait_edges(sweep):
        for side in range(2):
            for d in range(1, n_fold):
                forward(sweep, side, d, lax.rem(fold + n_fold - d, n_fold)).wait_recv()

    def whole_rows(read):
        parts = [read(f) for f in range(n_fold)]
        if rows % 16:
            return jnp.concatenate([part.astype(f32) for part in parts], axis=0).astype(bf16)
        return jnp.concatenate(parts, axis=0)

    def doubled(re, im):
        return jnp.concatenate(
            [jnp.concatenate([re, im], axis=1), jnp.concatenate([-im, re], axis=1)], axis=0)

    def stepped(alpha, start, moved):
        parts = [start(f).astype(f32) - turned(*alpha, moved(f).astype(f32)) for f in range(n_fold)]
        return jnp.concatenate(parts, axis=0).astype(bf16)

    def edge_chunks(alpha, side, q):
        folds = []
        for f in range(n_fold):
            start, moved = [unpack([rims[sweep, side, f, q, j].astype(f32) for j in range(6)])
                            if sweep == 0 or alpha is not None else None for sweep in range(2)]
            folds.append(start if alpha is None else [a - turned(*alpha, b) for a, b in zip(start, moved)])
        return [jnp.concatenate(parts, axis=0).astype(bf16) for parts in zip(*folds)]

    def build_local(alpha):
        def pair(h, carry):
            if alpha is None:
                chunks = [whole_rows(lambda f, i=i: gath[f, 2 * h + i]) for i in range(2)]
            else:
                chunks = []
                for g in (2 * h, 2 * h + 1):
                    res[g] = res[g] - turned(*alpha, first_image[fold, g])
                    chunks.append(stepped(alpha, lambda f, g=g: gath[f, g], lambda f, g=g: first_image[f, g]))
            (are, aim), (bre, bim) = [(c[:, :128], c[:, 128:]) for c in chunks]
            local_rhs[0, 2 * h] = doubled(are, aim)
            local_rhs[0, 2 * h + 1] = doubled(bre, bim)
            left = jnp.concatenate([jnp.concatenate([are, aim, bre, bim], axis=0),
                                    jnp.concatenate([bre, bim, are, aim], axis=0)], axis=1)
            moved = jnp.dot(left, moves[...], preferred_element_type=f32).astype(bf16)
            for i in range(2):
                for hop in range(4):
                    cut = moved[2 * comps * i:2 * comps * (i + 1), 128 * hop:128 * hop + 128]
                    local_rhs[1 + hop, 2 * h + i] = doubled(cut[:comps], cut[comps:])
            return carry

        lax.fori_loop(0, HALF, pair, 0, unroll=2)

    row_site = lax.broadcasted_iota(jnp.int32, (8, 256), 0)
    lane_site = lax.broadcasted_iota(jnp.int32, (8, 256), 1) % CHUNK
    upper = {bit: row_site // bit % 2 == 1 for bit in (4, 2, 1)}
    stays = {bit: row_site // bit % 2 == lane_site // bit % 2 for bit in (4, 2, 1)}

    def same_site(product):
        out = []
        for t in range(0, rows, 8):
            parts = [product[CHUNK * (t + r):CHUNK * (t + r + 1)] for r in range(8)]
            for bit in (4, 2, 1):
                merged = []
                for a, b in zip(parts[:bit], parts[bit:]):
                    here = jnp.where(upper[bit], b, a)
                    there = pltpu.roll(jnp.where(upper[bit], a, b), 4 if bit == 4 else bit, 0)
                    if bit != 4:
                        there = jnp.where(upper[bit], there, pltpu.roll(jnp.where(upper[bit], a, b), 8 - bit, 0))
                    merged.append(jnp.where(stays[bit], here, there))
                parts = merged
            out.append(parts[0])
        return out[0] if len(out) == 1 else jnp.concatenate(out, axis=0)

    def apply_local(begin, end):
        def chunk(g, carry):
            plane, x, low = g // HALF * HALF, g % HALF // 2, g % 2
            ahead, behind = plane + (x + 1) % 4 * 2 + low, plane + (x + 3) % 4 * 2 + low
            rhs = jnp.concatenate(
                [local_rhs[0, g], local_rhs[0, ahead], local_rhs[0, behind]]
                + [local_rhs[1 + hop, g] for hop in range(4)], axis=0)
            image[g] = same_site(jnp.dot(w_local[g], rhs, preferred_element_type=f32))
            return carry

        lax.fori_loop(begin, end, chunk, 0, unroll=end - begin)

    def dots(a, r):
        are, aim, rre, rim = a[:, :128], a[:, 128:], r[:, :128], r[:, 128:]
        return are * rre + aim * rim, are * rim - aim * rre, are * are + aim * aim

    def apply_across(alpha):
        def plane_chunk(h, after, before, sums):
            after = doubled(after[:, :128], after[:, 128:])
            before = doubled(before[:, :128], before[:, 128:])
            inner, outer = local_rhs[0, h], local_rhs[0, h + HALF]
            up = (outer.astype(f32) * live + after.astype(f32) * (1.0 - live)).astype(bf16)
            first = same_site(jnp.dot(w_across[h], jnp.concatenate([up, before], axis=0),
                                      preferred_element_type=f32))
            second = same_site(jnp.dot(w_across[h + HALF], jnp.concatenate([after, inner], axis=0),
                                       preferred_element_type=f32))
            first = first + image[h]
            second = (second + image[h + HALF]) * live
            if alpha is None:
                first_image[fold, h] = first
                first_image[fold, h + HALF] = second
            else:
                image[h] = first
                image[h + HALF] = second
            one, two = dots(first, res[h]), dots(second, res[h + HALF])
            return tuple(s + a + b for s, a, b in zip(sums, one, two))

        zero = jnp.zeros((rows, 128), f32)

        def group(q, sums):
            sides = [edge_chunks(alpha, side, q) for side in range(2)]
            for i in range(4):
                sums = plane_chunk(4 * q + i, sides[0][i], sides[1][i], sums)
            return sums

        return lax.fori_loop(0, 2, group, (zero, zero, zero))

    row8 = lax.broadcasted_iota(jnp.int32, (8, 128), 0)
    lane8 = lax.broadcasted_iota(jnp.int32, (8, 128), 1)

    def spread(value):
        for step in (4, 2, 1):
            value = value + jnp.where(lane8 // step % 2 == 0,
                                      pltpu.roll(value, 128 - step, 1), pltpu.roll(value, step, 1))
        return value

    def send_sums(sweep, sums):
        re, im, norm = [jnp.sum(s, axis=0, keepdims=True) for s in sums]
        value = spread(jnp.where(row8 == 0, re, jnp.where(row8 == 1, im, norm)))
        spot = lane8[:1] % CHUNK
        red[sweep, 0] = jnp.where(spot == 0, value[0:1], jnp.where(spot == 1, value[1:2], value[2:3]))

        def send(d, carry):
            pltpu.make_async_remote_copy(
                src_ref=red.at[sweep, 0], dst_ref=red.at[sweep, d],
                send_sem=s_send.at[sweep], recv_sem=s_recv.at[sweep],
                device_id=device(lax.rem(me + d, total)), device_id_type=MESH).start()
            return carry

        lax.fori_loop(1, total, send, 0, unroll=total <= 64)

    def wait_sums(sweep):
        everyone = red.at[sweep, pl.ds(1, total - 1)]
        pltpu.make_async_copy(everyone, everyone, s_recv.at[sweep]).wait()
        value = jnp.broadcast_to(jnp.sum(red[sweep], axis=0), (8, 128))
        value = spread(jnp.where(lane8 % CHUNK == row8, value, 0.0))
        norm = jnp.where(lane8[:1] < CHUNK * nrhs, value[2:3], 1.0)
        return value[0:1] / norm, value[1:2] / norm

    def natural(held, out):
        for p in range(2):
            for t in range(0, rows, 8):
                tiles = swap_blocks([held[g, t:t + 8, 128 * p:128 * p + 128] for g in range(GROUPS)])
                for k in range(nrhs):
                    out[p, k, t:t + 8] = tiles[k]

    copies = send_source()
    for hop in range(4):
        moves[:, 128 * hop:128 * hop + 128] = lane_moves(hop)
    for m in range(9):
        loads[m].wait()
        place = LOCAL.index(m) if m in LOCAL else ACROSS.index(m)
        target = w_local if m in LOCAL else w_across

        def two_rows(i, carry, m=m, place=place, target=target):
            flipped = []
            for a in range(2):
                both = jnp.concatenate([raw[m, 0, 2 * i + a], raw[m, 1, 2 * i + a]], axis=0)
                flipped.append(both.T.astype(f32))
            for g in range(GROUPS):
                piece = jnp.concatenate([f[8 * g:8 * g + 8] for f in flipped], axis=0)
                target[g, pl.ds(pl.multiple_of(16 * i, 16), 16),
                       2 * comps * place:2 * comps * (place + 1)] = piece.astype(bf16)
            return carry

        lax.fori_loop(0, rows // 2, two_rows, 0, unroll=min(rows // 2, 8))
    wait_gather(0, gath)
    build_local(None)
    copies += local_and_pass(0, copies[:2])
    send_sums(0, apply_across(None))
    later = send_image()
    first = wait_sums(0)
    wait_gather(1, first_image)
    build_local(first)
    later += local_and_pass(1, later[:2])
    send_sums(1, apply_across(first))
    natural(res, res_out)
    natural(image, image_out)
    second = wait_sums(1)
    alphas[...] = jnp.where(row8 == 0, first[0], jnp.where(row8 == 1, first[1], jnp.where(
        row8 == 2, second[0], jnp.where(row8 == 3, second[1], jnp.where(lane8 < 64, 1.0, live)))))
    for copy in copies + later:
        copy.wait_send()
    for sweep in range(SWEEPS):
        everyone = red.at[sweep, pl.ds(1, total - 1)]
        pltpu.make_async_copy(everyone, everyone, s_send.at[sweep]).wait()


def finish(source, res, image, alphas, sol_out, res_out):
    nrhs, rows = source.shape[1:3]
    f32 = jnp.float32
    kept = jnp.broadcast_to(alphas[4:5], (rows, 128))
    for k in range(nrhs):
        are, aim, bre, bim = [jnp.broadcast_to(alphas[i:i + 1, CHUNK * k:CHUNK * k + 1], (rows, 128))
                              for i in range(4)]
        sre, sim = [source[p, k].astype(f32) * kept for p in range(2)]
        rre, rim, ire, iim = res[0, k], res[1, k], image[0, k], image[1, k]
        sol_out[0, k] = (are * sre - aim * sim) + (bre * rre - bim * rim)
        sol_out[1, k] = (are * sim + aim * sre) + (bre * rim + bim * rre)
        res_out[0, k] = rre - (bre * ire - bim * iim)
        res_out[1, k] = rim - (bre * iim + bim * ire)


def body(n_grp, n_fold, blocks, source, plane_counts):
    rows, comps = blocks.shape[2], blocks.shape[3]
    nrhs = source.shape[2]
    bf16, f32 = jnp.bfloat16, jnp.float32
    shape = (2, nrhs, rows, GROUPS * CHUNK)
    vmem = pl.BlockSpec(memory_space=pltpu.VMEM)
    total = n_grp * n_fold
    held = jax.ShapeDtypeStruct(shape, f32)
    smem = pl.BlockSpec(memory_space=pltpu.SMEM)
    source = source.transpose(0, 2, 1, 3)
    iterate = pl.pallas_call(
        functools.partial(kernel, n_grp, n_fold),
        out_shape=(held, held, jax.ShapeDtypeStruct((8, 128), f32)),
        in_specs=[smem] + [pl.BlockSpec(memory_space=pltpu.HBM)] * 2,
        out_specs=(vmem, vmem, vmem),
        scratch_shapes=[
            pltpu.VMEM(source.shape, bf16),
            pltpu.VMEM((256, 512), bf16),
            pltpu.VMEM(blocks.shape, bf16),
            pltpu.VMEM((GROUPS, rows * CHUNK, len(LOCAL) * 2 * comps), bf16),
            pltpu.VMEM((GROUPS, rows * CHUNK, len(ACROSS) * 2 * comps), bf16),
            pltpu.VMEM((GROUPS, rows, 256), f32),
            pltpu.VMEM((GROUPS, rows, 256), f32),
            pltpu.VMEM((n_fold, GROUPS, rows, 256), f32),
            pltpu.VMEM((n_fold, GROUPS, rows, 256), bf16),
            pltpu.VMEM((SWEEPS, 2, 2, 6, rows, 128), bf16),
            pltpu.VMEM((SWEEPS, 2, n_fold, 2, 6, rows, 128), bf16),
            pltpu.VMEM((5, GROUPS, 2 * comps, 256), bf16),
            pltpu.VMEM((SWEEPS, total, 1, 128), f32),
            pltpu.SemaphoreType.DMA,
            pltpu.SemaphoreType.DMA((9,)),
            pltpu.SemaphoreType.DMA((SWEEPS, n_fold)),
            pltpu.SemaphoreType.DMA((SWEEPS, n_fold)),
            pltpu.SemaphoreType.DMA((SWEEPS, 2, n_fold)),
            pltpu.SemaphoreType.DMA((SWEEPS, 2, n_fold)),
            pltpu.SemaphoreType.DMA((SWEEPS,)),
            pltpu.SemaphoreType.DMA((SWEEPS,)),
        ],
        compiler_params=pltpu.CompilerParams(
            collective_id=0, has_side_effects=True, vmem_limit_bytes=52 * 1024 * 1024),
    )(plane_counts, blocks, pltpu.with_memory_space_constraint(source, pltpu.HBM))
    outs = pl.pallas_call(
        finish,
        out_shape=(jax.ShapeDtypeStruct(shape, f32), jax.ShapeDtypeStruct(shape, f32)),
        in_specs=[vmem] * 4,
        out_specs=(vmem, vmem),
        compiler_params=pltpu.CompilerParams(vmem_limit_bytes=8 * 1024 * 1024),
    )(source, *iterate)
    return tuple(out.transpose(0, 2, 1, 3) for out in outs)


def solution(mesh):
    return jax.shard_map(
        functools.partial(body, mesh.shape["grp"], mesh.shape["fold"]),
        mesh=mesh,
        in_specs=(P(None, None, "fold", None, "grp"), P(None, "fold", None, "grp"), P("grp")),
        out_specs=(P(None, "fold", None, "grp"), P(None, "fold", None, "grp")),
        check_vma=False,
    )
```

```python
import functools

import jax
import jax.numpy as jnp
import numpy as np
from jax import lax
from jax.experimental import pallas as pl
from jax.experimental.pallas import tpu as pltpu
from jax.sharding import PartitionSpec as P

SWEEPS = 2
CHUNK = 8
GROUPS = 16
HALF = GROUPS // 2
LOCAL = (0, 1, 2, 3, 4, 7, 8)
ACROSS = (5, 6)
MESH = pl.DeviceIdType.MESH


def lane_moves(hop):
    row = lax.broadcasted_iota(jnp.int32, (256, 128), 0)
    lane = lax.broadcasted_iota(jnp.int32, (256, 128), 1)
    base, site = lane // 8 * 8, lane % 8
    low, plane = site // 4 == 0, site // 4 * 4
    across = base + (site + 4) % 8
    origin = (jnp.where(low, across, across + 128), jnp.where(low, across + 128, across),
              base + plane + (site + 1) % 4, base + plane + (site + 3) % 4)[hop]
    return jnp.where(row == origin, 1.0, 0.0).astype(jnp.bfloat16)


def swap_blocks(tiles):
    tiles = list(tiles)
    block = lax.broadcasted_iota(jnp.int32, tiles[0].shape, 1) // CHUNK
    for bit in (1, 2, 4, 8):
        high = block // bit % 2 == 1
        for i in range(GROUPS):
            if i & bit == 0:
                a, b = tiles[i], tiles[i | bit]
                tiles[i] = jnp.where(high, pltpu.roll(b, CHUNK * bit, 1), a)
                tiles[i | bit] = jnp.where(high, b, pltpu.roll(a, 128 - CHUNK * bit, 1))
    return tiles


def pack(chunks):
    halves = [chunk[:, 128 * p:128 * p + 128] for chunk in chunks for p in range(2)]
    lane = lax.broadcasted_iota(jnp.int32, halves[0].shape, 1)
    return [jnp.where(lane < 96, halves[j], pltpu.roll(halves[6 + j // 3], 96 - 32 * (j % 3), 1)) for j in range(6)]


def unpack(tiles):
    lane = lax.broadcasted_iota(jnp.int32, tiles[0].shape, 1)
    halves = [jnp.where(lane < 96, tile, 0.0) for tile in tiles]
    for a, b, c in (tiles[:3], tiles[3:]):
        halves.append(jnp.where(lane < 32, pltpu.roll(a, 32, 1), jnp.where(
            lane < 64, pltpu.roll(b, 64, 1), jnp.where(lane < 96, pltpu.roll(c, 96, 1), 0.0))))
    return [jnp.concatenate(halves[2 * i:2 * i + 2], axis=1) for i in range(4)]


def turned(alpha_re, alpha_im, v):
    re, im = v[:, :128], v[:, 128:]
    return jnp.concatenate([alpha_re * re - alpha_im * im, alpha_re * im + alpha_im * re], axis=1)


def kernel(n_grp, n_fold, counts, blocks, source_hbm, res_out, image_out, alphas,
           source, moves, raw, w_local, w_across, image, res, first_image, gath, edge_pack, rims, local_rhs, red,
           source_sem, load_sem, x_send, x_recv, r_send, r_recv, s_send, s_recv):
    bf16, f32 = jnp.bfloat16, jnp.float32
    rows, comps = blocks.shape[2], blocks.shape[3]
    nrhs = source_hbm.shape[1]
    total = n_grp * n_fold
    grp, fold = lax.axis_index("grp"), lax.axis_index("fold")
    me = grp * n_fold + fold
    fetch = pltpu.make_async_copy(source_hbm, source, source_sem)
    fetch.start()
    loads = [pltpu.make_async_copy(blocks.at[m], raw.at[m], load_sem.at[m]) for m in range(9)]
    def device(index):
        return (lax.div(index, n_fold), lax.rem(index, n_fold))

    barrier = pltpu.get_barrier_semaphore()

    def greet(d, carry):
        pl.semaphore_signal(barrier, inc=1, device_id=device(lax.rem(me + d, total)), device_id_type=MESH)
        return carry

    lax.fori_loop(1, total, greet, 0, unroll=total <= 64)
    for load in loads:
        load.start()

    live = (counts[0] - 1).astype(f32)
    fetch.wait()

    for p in range(2):
        planes = [source[p, k].astype(f32) for k in range(nrhs)]
        for t in range(0, rows, 8):
            tiles = [plane[t:t + 8] for plane in planes]
            tiles += [jnp.zeros((8, 128), f32)] * (GROUPS - nrhs)
            for g, tile in enumerate(swap_blocks(tiles)):
                res[g, t:t + 8, 128 * p:128 * p + 128] = tile * live if g >= HALF else tile

    pl.semaphore_wait(barrier, total - 1)

    def send_edges(sweep, held):
        def group(q, carry):
            lower = [held(4 * q + i) for i in range(4)]
            upper = [held(4 * q + i + HALF) for i in range(4)]
            final = [b + a * (1.0 - live) for a, b in zip(lower, upper)]
            for side, chunks in enumerate((lower, final)):
                for j, tile in enumerate(pack(chunks)):
                    edge_pack[sweep, side, q, j] = tile.astype(bf16)
            return carry

        lax.fori_loop(0, 2, group, 0, unroll=2)
        copies = [pltpu.make_async_remote_copy(
            src_ref=edge_pack.at[sweep, side], dst_ref=rims.at[sweep, side, fold],
            send_sem=r_send.at[sweep, side, 0], recv_sem=r_recv.at[sweep, side, 0],
            device_id=(lax.rem(grp + step, n_grp), fold), device_id_type=MESH)
            for side, step in ((0, n_grp - 1), (1, 1))]
        for copy in copies:
            copy.start()
        return copies

    def send_gather(sweep, slots):
        copies = [pltpu.make_async_remote_copy(
            src_ref=slots.at[fold], dst_ref=slots.at[fold],
            send_sem=x_send.at[sweep, d], recv_sem=x_recv.at[sweep, d],
            device_id=(grp, lax.rem(fold + d, n_fold)), device_id_type=MESH) for d in range(1, n_fold)]
        for copy in copies:
            copy.start()
        return copies

    def send_source():
        edges = send_edges(0, lambda g: res[g])

        def fill(h, carry):
            gath[fold, h] = res[h].astype(bf16)
            return carry

        lax.fori_loop(0, GROUPS, fill, 0, unroll=4)
        return edges + send_gather(0, gath)

    def send_image():
        return send_edges(1, lambda g: first_image[fold, g]) + send_gather(1, first_image)

    def wait_gather(sweep, slots):
        for d in range(1, n_fold):
            slot = slots.at[lax.rem(fold + n_fold - d, n_fold)]
            pltpu.make_async_remote_copy(
                src_ref=slot, dst_ref=slot, send_sem=x_send.at[sweep, d], recv_sem=x_recv.at[sweep, d],
                device_id=(grp, lax.rem(fold + d, n_fold)), device_id_type=MESH).wait_recv()

    def forward(sweep, side, d, sender):
        slot = rims.at[sweep, side, sender]
        return pltpu.make_async_remote_copy(
            src_ref=slot, dst_ref=slot, send_sem=r_send.at[sweep, side, d],
            recv_sem=r_recv.at[sweep, side, d],
            device_id=(grp, lax.rem(fold + d, n_fold)), device_id_type=MESH)

    def pass_edge(sweep, side, edges):
        edges[side].wait_recv()
        passed = [forward(sweep, side, d, fold) for d in range(1, n_fold)]
        for copy in passed:
            copy.start()
        return passed

    def local_and_pass(sweep, edges):
        apply_local(0, 6)
        passed = pass_edge(sweep, 0, edges)
        apply_local(6, 10)
        passed += pass_edge(sweep, 1, edges)
        apply_local(10, 16)
        wait_edges(sweep)
        return passed

    def wait_edges(sweep):
        for side in range(2):
            for d in range(1, n_fold):
                forward(sweep, side, d, lax.rem(fold + n_fold - d, n_fold)).wait_recv()

    def whole_rows(read):
        parts = [read(f) for f in range(n_fold)]
        if rows % 16:
            return jnp.concatenate([part.astype(f32) for part in parts], axis=0).astype(bf16)
        return jnp.concatenate(parts, axis=0)

    def doubled(re, im):
        return jnp.concatenate(
            [jnp.concatenate([re, im], axis=1), jnp.concatenate([-im, re], axis=1)], axis=0)

    def stepped(alpha, start, moved):
        parts = [start(f).astype(f32) - turned(*alpha, moved(f).astype(f32)) for f in range(n_fold)]
        return jnp.concatenate(parts, axis=0).astype(bf16)

    def edge_chunks(alpha, side, q):
        folds = []
        for f in range(n_fold):
            start, moved = [unpack([rims[sweep, side, f, q, j].astype(f32) for j in range(6)])
                            if sweep == 0 or alpha is not None else None for sweep in range(2)]
            folds.append(start if alpha is None else [a - turned(*alpha, b) for a, b in zip(start, moved)])
        return [jnp.concatenate(parts, axis=0).astype(bf16) for parts in zip(*folds)]

    def build_local(alpha):
        def pair(h, carry):
            if alpha is None:
                chunks = [whole_rows(lambda f, i=i: gath[f, 2 * h + i]) for i in range(2)]
            else:
                chunks = []
                for g in (2 * h, 2 * h + 1):
                    res[g] = res[g] - turned(*alpha, first_image[fold, g])
                    chunks.append(stepped(alpha, lambda f, g=g: gath[f, g], lambda f, g=g: first_image[f, g]))
            (are, aim), (bre, bim) = [(c[:, :128], c[:, 128:]) for c in chunks]
            local_rhs[0, 2 * h] = doubled(are, aim)
            local_rhs[0, 2 * h + 1] = doubled(bre, bim)
            left = jnp.concatenate([jnp.concatenate([are, aim, bre, bim], axis=0),
                                    jnp.concatenate([bre, bim, are, aim], axis=0)], axis=1)
            moved = jnp.dot(left, moves[...], preferred_element_type=f32).astype(bf16)
            for i in range(2):
                for hop in range(4):
                    cut = moved[2 * comps * i:2 * comps * (i + 1), 128 * hop:128 * hop + 128]
                    local_rhs[1 + hop, 2 * h + i] = doubled(cut[:comps], cut[comps:])
            return carry

        lax.fori_loop(0, HALF, pair, 0, unroll=2)

    row_site = lax.broadcasted_iota(jnp.int32, (8, 256), 0)
    lane_site = lax.broadcasted_iota(jnp.int32, (8, 256), 1) % CHUNK
    upper = {bit: row_site // bit % 2 == 1 for bit in (4, 2, 1)}
    stays = {bit: row_site // bit % 2 == lane_site // bit % 2 for bit in (4, 2, 1)}

    def same_site(product):
        out = []
        for t in range(0, rows, 8):
            parts = [product[CHUNK * (t + r):CHUNK * (t + r + 1)] for r in range(8)]
            for bit in (4, 2, 1):
                merged = []
                for a, b in zip(parts[:bit], parts[bit:]):
                    here = jnp.where(upper[bit], b, a)
                    there = pltpu.roll(jnp.where(upper[bit], a, b), 4 if bit == 4 else bit, 0)
                    if bit != 4:
                        there = jnp.where(upper[bit], there, pltpu.roll(jnp.where(upper[bit], a, b), 8 - bit, 0))
                    merged.append(jnp.where(stays[bit], here, there))
                parts = merged
            out.append(parts[0])
        return out[0] if len(out) == 1 else jnp.concatenate(out, axis=0)

    def apply_local(begin, end):
        if begin < HALF < end:
            apply_local(begin, HALF)
            begin = HALF

        def chunk(g, carry):
            plane, x, low = g // HALF * HALF, g % HALF // 2, g % 2
            ahead, behind = plane + (x + 1) % 4 * 2 + low, plane + (x + 3) % 4 * 2 + low
            rhs = jnp.concatenate(
                [local_rhs[0, g], local_rhs[0, ahead], local_rhs[0, behind]]
                + [local_rhs[1 + hop, g] for hop in range(4)]
                + ([local_rhs[0, g - HALF]] if begin >= HALF else []), axis=0)
            weights = w_local[g]
            if begin >= HALF:
                weights = jnp.concatenate([weights, w_across[g, :, 2 * comps:]], axis=1)
            image[g] = same_site(jnp.dot(weights, rhs, preferred_element_type=f32))
            return carry

        lax.fori_loop(begin, end, chunk, 0, unroll=end - begin)

    def dots(a, r):
        are, aim, rre, rim = a[:, :128], a[:, 128:], r[:, :128], r[:, 128:]
        return are * rre + aim * rim, are * rim - aim * rre, are * are + aim * aim

    def apply_across(alpha):
        def plane_chunk(h, after, before, sums):
            after = doubled(after[:, :128], after[:, 128:])
            before = doubled(before[:, :128], before[:, 128:])
            outer = local_rhs[0, h + HALF]
            up = (outer.astype(f32) * live + after.astype(f32) * (1.0 - live)).astype(bf16)
            first = same_site(jnp.dot(w_across[h], jnp.concatenate([up, before], axis=0),
                                      preferred_element_type=f32))
            second = same_site(jnp.dot(w_across[h + HALF, :, :2 * comps], after, preferred_element_type=f32))
            first = first + image[h]
            second = (second + image[h + HALF]) * live
            if alpha is None:
                first_image[fold, h] = first
                first_image[fold, h + HALF] = second
            else:
                image[h] = first
                image[h + HALF] = second
            one, two = dots(first, res[h]), dots(second, res[h + HALF])
            return tuple(s + a + b for s, a, b in zip(sums, one, two))

        zero = jnp.zeros((rows, 128), f32)

        def group(q, sums):
            sides = [edge_chunks(alpha, side, q) for side in range(2)]
            for i in range(4):
                sums = plane_chunk(4 * q + i, sides[0][i], sides[1][i], sums)
            return sums

        return lax.fori_loop(0, 2, group, (zero, zero, zero))

    row8 = lax.broadcasted_iota(jnp.int32, (8, 128), 0)
    lane8 = lax.broadcasted_iota(jnp.int32, (8, 128), 1)

    def spread(value):
        for step in (4, 2, 1):
            value = value + jnp.where(lane8 // step % 2 == 0,
                                      pltpu.roll(value, 128 - step, 1), pltpu.roll(value, step, 1))
        return value

    def send_sums(sweep, sums):
        re, im, norm = [jnp.sum(s, axis=0, keepdims=True) for s in sums]
        value = spread(jnp.where(row8 == 0, re, jnp.where(row8 == 1, im, norm)))
        spot = lane8[:1] % CHUNK
        red[sweep, 0] = jnp.where(spot == 0, value[0:1], jnp.where(spot == 1, value[1:2], value[2:3]))

        def send(d, carry):
            pltpu.make_async_remote_copy(
                src_ref=red.at[sweep, 0], dst_ref=red.at[sweep, d],
                send_sem=s_send.at[sweep], recv_sem=s_recv.at[sweep],
                device_id=device(lax.rem(me + d, total)), device_id_type=MESH).start()
            return carry

        lax.fori_loop(1, total, send, 0, unroll=total <= 64)

    def wait_sent(sweep):
        everyone = red.at[sweep, pl.ds(1, total - 1)]
        pltpu.make_async_copy(everyone, everyone, s_send.at[sweep]).wait()

    def wait_sums(sweep):
        everyone = red.at[sweep, pl.ds(1, total - 1)]
        pltpu.make_async_copy(everyone, everyone, s_recv.at[sweep]).wait()
        value = jnp.broadcast_to(jnp.sum(red[sweep], axis=0), (8, 128))
        value = spread(jnp.where(lane8 % CHUNK == row8, value, 0.0))
        norm = jnp.where(lane8[:1] < CHUNK * nrhs, value[2:3], 1.0)
        return value[0:1] / norm, value[1:2] / norm

    def natural(held, out):
        for p in range(2):
            for t in range(0, rows, 8):
                tiles = swap_blocks([held[g, t:t + 8, 128 * p:128 * p + 128] for g in range(GROUPS)])
                for k in range(nrhs):
                    out[p, k, t:t + 8] = tiles[k]

    copies = send_source()
    for hop in range(4):
        moves[:, 128 * hop:128 * hop + 128] = lane_moves(hop)
    for m in range(9):
        loads[m].wait()
        place = LOCAL.index(m) if m in LOCAL else ACROSS.index(m)
        target = w_local if m in LOCAL else w_across

        def two_rows(i, carry, m=m, place=place, target=target):
            flipped = []
            for a in range(2):
                both = jnp.concatenate([raw[m, 0, 2 * i + a], raw[m, 1, 2 * i + a]], axis=0)
                flipped.append(both.T.astype(f32))
            for g in range(GROUPS):
                piece = jnp.concatenate([f[8 * g:8 * g + 8] for f in flipped], axis=0)
                target[g, pl.ds(pl.multiple_of(16 * i, 16), 16),
                       2 * comps * place:2 * comps * (place + 1)] = piece.astype(bf16)
            return carry

        lax.fori_loop(0, rows // 2, two_rows, 0, unroll=min(rows // 2, 8))
    wait_gather(0, gath)
    build_local(None)
    copies += local_and_pass(0, copies[:2])
    send_sums(0, apply_across(None))
    later = send_image()
    first = wait_sums(0)
    wait_gather(1, first_image)
    build_local(first)
    later += local_and_pass(1, later[:2])
    send_sums(1, apply_across(first))
    natural(res, res_out)
    natural(image, image_out)
    for copy in copies + later:
        copy.wait_send()
    wait_sent(0)
    second = wait_sums(1)
    alphas[...] = jnp.where(row8 == 0, first[0], jnp.where(row8 == 1, first[1], jnp.where(
        row8 == 2, second[0], jnp.where(row8 == 3, second[1], jnp.where(lane8 < 64, 1.0, live)))))
    wait_sent(1)


def finish(source, res, image, alphas, sol_out, res_out):
    nrhs, rows = source.shape[1:3]
    f32 = jnp.float32
    kept = jnp.broadcast_to(alphas[4:5], (rows, 128))
    for k in range(nrhs):
        are, aim, bre, bim = [jnp.broadcast_to(alphas[i:i + 1, CHUNK * k:CHUNK * k + 1], (rows, 128))
                              for i in range(4)]
        sre, sim = [source[p, k].astype(f32) * kept for p in range(2)]
        rre, rim, ire, iim = res[0, k], res[1, k], image[0, k], image[1, k]
        sol_out[0, k] = (are * sre - aim * sim) + (bre * rre - bim * rim)
        sol_out[1, k] = (are * sim + aim * sre) + (bre * rim + bim * rre)
        res_out[0, k] = rre - (bre * ire - bim * iim)
        res_out[1, k] = rim - (bre * iim + bim * ire)


def body(n_grp, n_fold, blocks, source, plane_counts):
    rows, comps = blocks.shape[2], blocks.shape[3]
    nrhs = source.shape[2]
    bf16, f32 = jnp.bfloat16, jnp.float32
    shape = (2, nrhs, rows, GROUPS * CHUNK)
    vmem = pl.BlockSpec(memory_space=pltpu.VMEM)
    total = n_grp * n_fold
    held = jax.ShapeDtypeStruct(shape, f32)
    smem = pl.BlockSpec(memory_space=pltpu.SMEM)
    source = source.transpose(0, 2, 1, 3)
    iterate = pl.pallas_call(
        functools.partial(kernel, n_grp, n_fold),
        out_shape=(held, held, jax.ShapeDtypeStruct((8, 128), f32)),
        in_specs=[smem] + [pl.BlockSpec(memory_space=pltpu.HBM)] * 2,
        out_specs=(vmem, vmem, vmem),
        scratch_shapes=[
            pltpu.VMEM(source.shape, bf16),
            pltpu.VMEM((256, 512), bf16),
            pltpu.VMEM(blocks.shape, bf16),
            pltpu.VMEM((GROUPS, rows * CHUNK, len(LOCAL) * 2 * comps), bf16),
            pltpu.VMEM((GROUPS, rows * CHUNK, len(ACROSS) * 2 * comps), bf16),
            pltpu.VMEM((GROUPS, rows, 256), f32),
            pltpu.VMEM((GROUPS, rows, 256), f32),
            pltpu.VMEM((n_fold, GROUPS, rows, 256), f32),
            pltpu.VMEM((n_fold, GROUPS, rows, 256), bf16),
            pltpu.VMEM((SWEEPS, 2, 2, 6, rows, 128), bf16),
            pltpu.VMEM((SWEEPS, 2, n_fold, 2, 6, rows, 128), bf16),
            pltpu.VMEM((5, GROUPS, 2 * comps, 256), bf16),
            pltpu.VMEM((SWEEPS, total, 1, 128), f32),
            pltpu.SemaphoreType.DMA,
            pltpu.SemaphoreType.DMA((9,)),
            pltpu.SemaphoreType.DMA((SWEEPS, n_fold)),
            pltpu.SemaphoreType.DMA((SWEEPS, n_fold)),
            pltpu.SemaphoreType.DMA((SWEEPS, 2, n_fold)),
            pltpu.SemaphoreType.DMA((SWEEPS, 2, n_fold)),
            pltpu.SemaphoreType.DMA((SWEEPS,)),
            pltpu.SemaphoreType.DMA((SWEEPS,)),
        ],
        compiler_params=pltpu.CompilerParams(
            collective_id=0, has_side_effects=True, vmem_limit_bytes=52 * 1024 * 1024),
    )(plane_counts, blocks, pltpu.with_memory_space_constraint(source, pltpu.HBM))
    outs = pl.pallas_call(
        finish,
        out_shape=(jax.ShapeDtypeStruct(shape, f32), jax.ShapeDtypeStruct(shape, f32)),
        in_specs=[vmem] * 4,
        out_specs=(vmem, vmem),
        compiler_params=pltpu.CompilerParams(vmem_limit_bytes=8 * 1024 * 1024),
    )(source, *iterate)
    return tuple(out.transpose(0, 2, 1, 3) for out in outs)


def solution(mesh):
    return jax.shard_map(
        functools.partial(body, mesh.shape["grp"], mesh.shape["fold"]),
        mesh=mesh,
        in_specs=(P(None, None, "fold", None, "grp"), P(None, "fold", None, "grp"), P("grp")),
        out_specs=(P(None, "fold", None, "grp"), P(None, "fold", None, "grp")),
        check_vma=False,
    )
```

```python
import functools

import jax
import jax.numpy as jnp
import numpy as np
from jax import lax
from jax.experimental import pallas as pl
from jax.experimental.pallas import tpu as pltpu
from jax.sharding import PartitionSpec as P

SWEEPS = 2
CHUNK = 8
GROUPS = 16
HALF = GROUPS // 2
LOCAL = (0, 1, 2, 3, 4, 7, 8)
ACROSS = (5, 6)
MESH = pl.DeviceIdType.MESH


def lane_moves(hop):
    row = lax.broadcasted_iota(jnp.int32, (256, 128), 0)
    lane = lax.broadcasted_iota(jnp.int32, (256, 128), 1)
    base, site = lane // 8 * 8, lane % 8
    low, plane = site // 4 == 0, site // 4 * 4
    across = base + (site + 4) % 8
    origin = (jnp.where(low, across, across + 128), jnp.where(low, across + 128, across),
              base + plane + (site + 1) % 4, base + plane + (site + 3) % 4)[hop]
    return jnp.where(row == origin, 1.0, 0.0).astype(jnp.bfloat16)


def swap_blocks(tiles):
    tiles = list(tiles)
    block = lax.broadcasted_iota(jnp.int32, tiles[0].shape, 1) // CHUNK
    for bit in (1, 2, 4, 8):
        high = block // bit % 2 == 1
        for i in range(GROUPS):
            if i & bit == 0:
                a, b = tiles[i], tiles[i | bit]
                tiles[i] = jnp.where(high, pltpu.roll(b, CHUNK * bit, 1), a)
                tiles[i | bit] = jnp.where(high, b, pltpu.roll(a, 128 - CHUNK * bit, 1))
    return tiles


def pack(chunks):
    halves = [chunk[:, 128 * p:128 * p + 128] for chunk in chunks for p in range(2)]
    lane = lax.broadcasted_iota(jnp.int32, halves[0].shape, 1)
    return [jnp.where(lane < 96, halves[j], pltpu.roll(halves[6 + j // 3], 96 - 32 * (j % 3), 1)) for j in range(6)]


def unpack(tiles):
    lane = lax.broadcasted_iota(jnp.int32, tiles[0].shape, 1)
    halves = [jnp.where(lane < 96, tile, 0.0) for tile in tiles]
    for a, b, c in (tiles[:3], tiles[3:]):
        halves.append(jnp.where(lane < 32, pltpu.roll(a, 32, 1), jnp.where(
            lane < 64, pltpu.roll(b, 64, 1), jnp.where(lane < 96, pltpu.roll(c, 96, 1), 0.0))))
    return [jnp.concatenate(halves[2 * i:2 * i + 2], axis=1) for i in range(4)]


def turned(alpha_re, alpha_im, v):
    re, im = v[:, :128], v[:, 128:]
    return jnp.concatenate([alpha_re * re - alpha_im * im, alpha_re * im + alpha_im * re], axis=1)


def kernel(n_grp, n_fold, counts, blocks, source_hbm, res_out, image_out, alphas,
           source, moves, raw, w_local, w_across, image, res, first_image, gath, edge_pack, rims, local_rhs, red,
           source_sem, load_sem, x_send, x_recv, r_send, r_recv, s_send, s_recv):
    bf16, f32 = jnp.bfloat16, jnp.float32
    rows, comps = blocks.shape[2], blocks.shape[3]
    nrhs = source_hbm.shape[1]
    total = n_grp * n_fold
    grp, fold = lax.axis_index("grp"), lax.axis_index("fold")
    me = grp * n_fold + fold
    fetch = pltpu.make_async_copy(source_hbm, source, source_sem)
    fetch.start()
    loads = [pltpu.make_async_copy(blocks.at[m], raw.at[m], load_sem.at[m]) for m in range(9)]
    def device(index):
        return (lax.div(index, n_fold), lax.rem(index, n_fold))

    barrier = pltpu.get_barrier_semaphore()

    def greet(d, carry):
        pl.semaphore_signal(barrier, inc=1, device_id=device(lax.rem(me + d, total)), device_id_type=MESH)
        return carry

    lax.fori_loop(1, total, greet, 0, unroll=total <= 64)
    for load in loads:
        load.start()

    live = (counts[0] - 1).astype(f32)
    fetch.wait()

    for p in range(2):
        planes = [source[p, k].astype(f32) for k in range(nrhs)]
        for t in range(0, rows, 8):
            tiles = [plane[t:t + 8] for plane in planes]
            tiles += [jnp.zeros((8, 128), f32)] * (GROUPS - nrhs)
            for g, tile in enumerate(swap_blocks(tiles)):
                res[g, t:t + 8, 128 * p:128 * p + 128] = tile * live if g >= HALF else tile

    pl.semaphore_wait(barrier, total - 1)

    def send_edges(sweep, held):
        def group(q, carry):
            lower = [held(4 * q + i) for i in range(4)]
            upper = [held(4 * q + i + HALF) for i in range(4)]
            final = [b + a * (1.0 - live) for a, b in zip(lower, upper)]
            for side, chunks in enumerate((lower, final)):
                for j, tile in enumerate(pack(chunks)):
                    edge_pack[sweep, side, q, j] = tile.astype(bf16)
            return carry

        lax.fori_loop(0, 2, group, 0, unroll=2)
        copies = [pltpu.make_async_remote_copy(
            src_ref=edge_pack.at[sweep, side], dst_ref=rims.at[sweep, side, fold],
            send_sem=r_send.at[sweep, side, 0], recv_sem=r_recv.at[sweep, side, 0],
            device_id=(lax.rem(grp + step, n_grp), fold), device_id_type=MESH)
            for side, step in ((0, n_grp - 1), (1, 1))]
        for copy in copies:
            copy.start()
        return copies

    def send_gather(sweep, slots):
        copies = [pltpu.make_async_remote_copy(
            src_ref=slots.at[fold], dst_ref=slots.at[fold],
            send_sem=x_send.at[sweep, d], recv_sem=x_recv.at[sweep, d],
            device_id=(grp, lax.rem(fold + d, n_fold)), device_id_type=MESH) for d in range(1, n_fold)]
        for copy in copies:
            copy.start()
        return copies

    def send_source():
        edges = send_edges(0, lambda g: res[g])

        def fill(h, carry):
            gath[fold, h] = res[h].astype(bf16)
            return carry

        lax.fori_loop(0, GROUPS, fill, 0, unroll=4)
        return edges + send_gather(0, gath)

    def send_image():
        return send_edges(1, lambda g: first_image[fold, g]) + send_gather(1, first_image)

    def wait_gather(sweep, slots):
        for d in range(1, n_fold):
            slot = slots.at[lax.rem(fold + n_fold - d, n_fold)]
            pltpu.make_async_remote_copy(
                src_ref=slot, dst_ref=slot, send_sem=x_send.at[sweep, d], recv_sem=x_recv.at[sweep, d],
                device_id=(grp, lax.rem(fold + d, n_fold)), device_id_type=MESH).wait_recv()

    def forward(sweep, side, d, sender):
        slot = rims.at[sweep, side, sender]
        return pltpu.make_async_remote_copy(
            src_ref=slot, dst_ref=slot, send_sem=r_send.at[sweep, side, d],
            recv_sem=r_recv.at[sweep, side, d],
            device_id=(grp, lax.rem(fold + d, n_fold)), device_id_type=MESH)

    def pass_edge(sweep, side, edges):
        edges[side].wait_recv()
        passed = [forward(sweep, side, d, fold) for d in range(1, n_fold)]
        for copy in passed:
            copy.start()
        return passed

    def local_and_pass(sweep, edges):
        apply_local(0, 6)
        passed = pass_edge(sweep, 0, edges)
        apply_local(6, 10)
        passed += pass_edge(sweep, 1, edges)
        apply_local(10, 16)
        wait_edges(sweep)
        return passed

    def wait_edges(sweep):
        for side in range(2):
            for d in range(1, n_fold):
                forward(sweep, side, d, lax.rem(fold + n_fold - d, n_fold)).wait_recv()

    def whole_rows(read):
        parts = [read(f) for f in range(n_fold)]
        if rows % 16:
            return jnp.concatenate([part.astype(f32) for part in parts], axis=0).astype(bf16)
        return jnp.concatenate(parts, axis=0)

    def doubled(re, im):
        return jnp.concatenate(
            [jnp.concatenate([re, im], axis=1), jnp.concatenate([-im, re], axis=1)], axis=0)

    def stepped(alpha, start, moved):
        parts = [start(f).astype(f32) - turned(*alpha, moved(f).astype(f32)) for f in range(n_fold)]
        return jnp.concatenate(parts, axis=0).astype(bf16)

    def edge_chunks(alpha, side, q):
        folds = []
        for f in range(n_fold):
            start, moved = [unpack([rims[sweep, side, f, q, j].astype(f32) for j in range(6)])
                            if sweep == 0 or alpha is not None else None for sweep in range(2)]
            folds.append(start if alpha is None else [a - turned(*alpha, b) for a, b in zip(start, moved)])
        return [jnp.concatenate(parts, axis=0).astype(bf16) for parts in zip(*folds)]

    def build_local(alpha):
        def pair(h, carry):
            if alpha is None:
                chunks = [whole_rows(lambda f, i=i: gath[f, 2 * h + i]) for i in range(2)]
            else:
                chunks = []
                for g in (2 * h, 2 * h + 1):
                    res[g] = res[g] - turned(*alpha, first_image[fold, g])
                    chunks.append(stepped(alpha, lambda f, g=g: gath[f, g], lambda f, g=g: first_image[f, g]))
            (are, aim), (bre, bim) = [(c[:, :128], c[:, 128:]) for c in chunks]
            local_rhs[0, 2 * h] = doubled(are, aim)
            local_rhs[0, 2 * h + 1] = doubled(bre, bim)
            left = jnp.concatenate([jnp.concatenate([are, aim, bre, bim], axis=0),
                                    jnp.concatenate([bre, bim, are, aim], axis=0)], axis=1)
            moved = jnp.dot(left, moves[...], preferred_element_type=f32).astype(bf16)
            for i in range(2):
                for hop in range(4):
                    cut = moved[2 * comps * i:2 * comps * (i + 1), 128 * hop:128 * hop + 128]
                    local_rhs[1 + hop, 2 * h + i] = doubled(cut[:comps], cut[comps:])
            return carry

        lax.fori_loop(0, HALF, pair, 0, unroll=2)

    row_site = lax.broadcasted_iota(jnp.int32, (8, 256), 0)
    lane_site = lax.broadcasted_iota(jnp.int32, (8, 256), 1) % CHUNK
    upper = {bit: row_site // bit % 2 == 1 for bit in (4, 2, 1)}
    stays = {bit: row_site // bit % 2 == lane_site // bit % 2 for bit in (4, 2, 1)}

    def same_site(product):
        out = []
        for t in range(0, rows, 8):
            parts = [product[CHUNK * (t + r):CHUNK * (t + r + 1)] for r in range(8)]
            for bit in (4, 2, 1):
                merged = []
                for a, b in zip(parts[:bit], parts[bit:]):
                    here = jnp.where(upper[bit], b, a)
                    there = pltpu.roll(jnp.where(upper[bit], a, b), 4 if bit == 4 else bit, 0)
                    if bit != 4:
                        there = jnp.where(upper[bit], there, pltpu.roll(jnp.where(upper[bit], a, b), 8 - bit, 0))
                    merged.append(jnp.where(stays[bit], here, there))
                parts = merged
            out.append(parts[0])
        return out[0] if len(out) == 1 else jnp.concatenate(out, axis=0)

    def apply_local(begin, end):
        def chunk(g, carry):
            plane, x, low = g // HALF * HALF, g % HALF // 2, g % 2
            ahead, behind = plane + (x + 1) % 4 * 2 + low, plane + (x + 3) % 4 * 2 + low
            rhs = jnp.concatenate(
                [local_rhs[0, g], local_rhs[0, ahead], local_rhs[0, behind]]
                + [local_rhs[1 + hop, g] for hop in range(4)], axis=0)
            image[g] = same_site(jnp.dot(w_local[g], rhs, preferred_element_type=f32))
            return carry

        lax.fori_loop(begin, end, chunk, 0, unroll=end - begin)

    def dots(a, r):
        are, aim, rre, rim = a[:, :128], a[:, 128:], r[:, :128], r[:, 128:]
        return are * rre + aim * rim, are * rim - aim * rre, are * are + aim * aim

    def apply_across(alpha):
        def plane_chunk(h, after, before, sums):
            after = doubled(after[:, :128], after[:, 128:])
            before = doubled(before[:, :128], before[:, 128:])
            inner, outer = local_rhs[0, h], local_rhs[0, h + HALF]
            up = (outer.astype(f32) * live + after.astype(f32) * (1.0 - live)).astype(bf16)
            first = same_site(jnp.dot(w_across[h], jnp.concatenate([up, before], axis=0),
                                      preferred_element_type=f32))
            second = same_site(jnp.dot(w_across[h + HALF], jnp.concatenate([after, inner], axis=0),
                                       preferred_element_type=f32))
            first = first + image[h]
            second = (second + image[h + HALF]) * live
            if alpha is None:
                first_image[fold, h] = first
                first_image[fold, h + HALF] = second
            else:
                image[h] = first
                image[h + HALF] = second
            one, two = dots(first, res[h]), dots(second, res[h + HALF])
            return tuple(s + a + b for s, a, b in zip(sums, one, two))

        zero = jnp.zeros((rows, 128), f32)

        def group(q, sums):
            sides = [edge_chunks(alpha, side, q) for side in range(2)]
            for i in range(4):
                sums = plane_chunk(4 * q + i, sides[0][i], sides[1][i], sums)
            return sums

        return lax.fori_loop(0, 2, group, (zero, zero, zero))

    row8 = lax.broadcasted_iota(jnp.int32, (8, 128), 0)
    lane8 = lax.broadcasted_iota(jnp.int32, (8, 128), 1)

    def spread(value):
        for step in (4, 2, 1):
            value = value + jnp.where(lane8 // step % 2 == 0,
                                      pltpu.roll(value, 128 - step, 1), pltpu.roll(value, step, 1))
        return value

    def send_sums(sweep, sums):
        re, im, norm = [jnp.sum(s, axis=0, keepdims=True) for s in sums]
        value = spread(jnp.where(row8 == 0, re, jnp.where(row8 == 1, im, norm)))
        spot = lane8[:1] % CHUNK
        red[sweep, 0] = jnp.where(spot == 0, value[0:1], jnp.where(spot == 1, value[1:2], value[2:3]))

        def send(d, carry):
            pltpu.make_async_remote_copy(
                src_ref=red.at[sweep, 0], dst_ref=red.at[sweep, d],
                send_sem=s_send.at[sweep], recv_sem=s_recv.at[sweep],
                device_id=device(lax.rem(me + d, total)), device_id_type=MESH).start()
            return carry

        lax.fori_loop(1, total, send, 0, unroll=total <= 64)

    def wait_sent(sweep):
        everyone = red.at[sweep, pl.ds(1, total - 1)]
        pltpu.make_async_copy(everyone, everyone, s_send.at[sweep]).wait()

    def wait_sums(sweep):
        everyone = red.at[sweep, pl.ds(1, total - 1)]
        pltpu.make_async_copy(everyone, everyone, s_recv.at[sweep]).wait()
        value = jnp.broadcast_to(jnp.sum(red[sweep], axis=0), (8, 128))
        value = spread(jnp.where(lane8 % CHUNK == row8, value, 0.0))
        norm = jnp.where(lane8[:1] < CHUNK * nrhs, value[2:3], 1.0)
        return value[0:1] / norm, value[1:2] / norm

    def natural(held, out):
        for p in range(2):
            for t in range(0, rows, 8):
                tiles = swap_blocks([held[g, t:t + 8, 128 * p:128 * p + 128] for g in range(GROUPS)])
                for k in range(nrhs):
                    out[p, k, t:t + 8] = tiles[k]

    copies = send_source()
    for hop in range(4):
        moves[:, 128 * hop:128 * hop + 128] = lane_moves(hop)
    for m in range(9):
        loads[m].wait()
        place = LOCAL.index(m) if m in LOCAL else ACROSS.index(m)
        target = w_local if m in LOCAL else w_across

        def two_rows(i, carry, m=m, place=place, target=target):
            flipped = []
            for a in range(2):
                both = jnp.concatenate([raw[m, 0, 2 * i + a], raw[m, 1, 2 * i + a]], axis=0)
                flipped.append(both.T.astype(f32))
            for g in range(GROUPS):
                piece = jnp.concatenate([f[8 * g:8 * g + 8] for f in flipped], axis=0)
                target[g, pl.ds(pl.multiple_of(16 * i, 16), 16),
                       2 * comps * place:2 * comps * (place + 1)] = piece.astype(bf16)
            return carry

        lax.fori_loop(0, rows // 2, two_rows, 0, unroll=min(rows // 2, 8))
    wait_gather(0, gath)
    build_local(None)
    copies += local_and_pass(0, copies[:2])
    send_sums(0, apply_across(None))
    later = send_image()
    first = wait_sums(0)
    wait_gather(1, first_image)
    build_local(first)
    later += local_and_pass(1, later[:2])
    send_sums(1, apply_across(first))
    natural(res, res_out)
    natural(image, image_out)
    for copy in copies + later:
        copy.wait_send()
    wait_sent(0)
    second = wait_sums(1)
    alphas[...] = jnp.where(row8 == 0, first[0], jnp.where(row8 == 1, first[1], jnp.where(
        row8 == 2, second[0], jnp.where(row8 == 3, second[1], jnp.where(lane8 < 64, 1.0, live)))))
    wait_sent(1)


def finish(source, res, image, alphas, sol_out, res_out):
    nrhs, rows = source.shape[1:3]
    f32 = jnp.float32
    kept = jnp.broadcast_to(alphas[4:5], (rows, 128))
    for k in range(nrhs):
        are, aim, bre, bim = [jnp.broadcast_to(alphas[i:i + 1, CHUNK * k:CHUNK * k + 1], (rows, 128))
                              for i in range(4)]
        sre, sim = [source[p, k].astype(f32) * kept for p in range(2)]
        rre, rim, ire, iim = res[0, k], res[1, k], image[0, k], image[1, k]
        sol_out[0, k] = (are * sre - aim * sim) + (bre * rre - bim * rim)
        sol_out[1, k] = (are * sim + aim * sre) + (bre * rim + bim * rre)
        res_out[0, k] = rre - (bre * ire - bim * iim)
        res_out[1, k] = rim - (bre * iim + bim * ire)


def body(n_grp, n_fold, blocks, source, plane_counts):
    rows, comps = blocks.shape[2], blocks.shape[3]
    nrhs = source.shape[2]
    bf16, f32 = jnp.bfloat16, jnp.float32
    shape = (2, nrhs, rows, GROUPS * CHUNK)
    vmem = pl.BlockSpec(memory_space=pltpu.VMEM)
    total = n_grp * n_fold
    held = jax.ShapeDtypeStruct(shape, f32)
    smem = pl.BlockSpec(memory_space=pltpu.SMEM)
    source = source.transpose(0, 2, 1, 3)
    iterate = pl.pallas_call(
        functools.partial(kernel, n_grp, n_fold),
        out_shape=(held, held, jax.ShapeDtypeStruct((8, 128), f32)),
        in_specs=[smem] + [pl.BlockSpec(memory_space=pltpu.HBM)] * 2,
        out_specs=(vmem, vmem, vmem),
        scratch_shapes=[
            pltpu.VMEM(source.shape, bf16),
            pltpu.VMEM((256, 512), bf16),
            pltpu.VMEM(blocks.shape, bf16),
            pltpu.VMEM((GROUPS, rows * CHUNK, len(LOCAL) * 2 * comps), bf16),
            pltpu.VMEM((GROUPS, rows * CHUNK, len(ACROSS) * 2 * comps), bf16),
            pltpu.VMEM((GROUPS, rows, 256), f32),
            pltpu.VMEM((GROUPS, rows, 256), f32),
            pltpu.VMEM((n_fold, GROUPS, rows, 256), f32),
            pltpu.VMEM((n_fold, GROUPS, rows, 256), bf16),
            pltpu.VMEM((SWEEPS, 2, 2, 6, rows, 128), bf16),
            pltpu.VMEM((SWEEPS, 2, n_fold, 2, 6, rows, 128), bf16),
            pltpu.VMEM((5, GROUPS, 2 * comps, 256), bf16),
            pltpu.VMEM((SWEEPS, total, 1, 128), f32),
            pltpu.SemaphoreType.DMA,
            pltpu.SemaphoreType.DMA((9,)),
            pltpu.SemaphoreType.DMA((SWEEPS, n_fold)),
            pltpu.SemaphoreType.DMA((SWEEPS, n_fold)),
            pltpu.SemaphoreType.DMA((SWEEPS, 2, n_fold)),
            pltpu.SemaphoreType.DMA((SWEEPS, 2, n_fold)),
            pltpu.SemaphoreType.DMA((SWEEPS,)),
            pltpu.SemaphoreType.DMA((SWEEPS,)),
        ],
        compiler_params=pltpu.CompilerParams(
            collective_id=0, has_side_effects=True, vmem_limit_bytes=52 * 1024 * 1024),
    )(plane_counts, blocks, pltpu.with_memory_space_constraint(source, pltpu.HBM))
    outs = pl.pallas_call(
        finish,
        out_shape=(jax.ShapeDtypeStruct(shape, f32), jax.ShapeDtypeStruct(shape, f32)),
        in_specs=[vmem] * 4,
        out_specs=(vmem, vmem),
        compiler_params=pltpu.CompilerParams(vmem_limit_bytes=8 * 1024 * 1024),
    )(source, *iterate)
    return tuple(out.transpose(0, 2, 1, 3) for out in outs)


def solution(mesh):
    return jax.shard_map(
        functools.partial(body, mesh.shape["grp"], mesh.shape["fold"]),
        mesh=mesh,
        in_specs=(P(None, None, "fold", None, "grp"), P(None, "fold", None, "grp"), P("grp")),
        out_specs=(P(None, "fold", None, "grp"), P(None, "fold", None, "grp")),
        check_vma=False,
    )
```
